1024 devices in a mesh: hi: 16 (over y_hi, x, core), lo: 64 (over y_lo, z).
Axes of the slice: x: 4, y: 4 (y_hi: 2, y_lo: 2; y = y_hi * 2 + y_lo), z: 32, core: 2. Of those that a mesh axis runs over, the one named last changes fastest.
Arguments:
- ket_state: float32 [2, 16777216], P(None, ('hi', 'lo')), may hold values from -6 to 6
- bra_state: float32 [2, 16777216], P(None, ('hi', 'lo')), may hold values from -6 to 6
- gate_matrices: float32 [5, 64, 128], replicated, may hold values from -0.5 to 0.5
Outputs:
- ket_out: float32 [2, 16777216], P(None, ('hi', 'lo'))
- bra_out: float32 [2, 16777216], P(None, ('hi', 'lo'))
- gradient: float32 [5, 64, 128], P(None, 'lo')
The draws below stay inside these ranges and needn't reach their ends.
All inputs are finite; a program needn't handle non-finite values.
Results may differ from the reference program's by a relative error of at most 0.0001.
Values sent between devices are 32-bit elements; how exact they have to be, the bound alone decides.
A program may use at most 64 MiB of HBM per device.

```python
import jax
import jax.numpy as jnp
from jax import lax

AMP_DEV = 16384
GATE = 64
LAYERS = 5
AMPS = 16777216
N_HI = 16
N_LO = 64


def steps_of(own_key, shape, pieces, least, high):
    factor_of = 1.0
    for position, shards_of in pieces:
        steps = jax.random.uniform(jax.random.fold_in(jax.random.fold_in(own_key, 6), position), (shards_of,), jnp.float32, least / len(pieces), high / len(pieces))
        factor_of = factor_of * jnp.repeat(jnp.exp(steps), shape[position] // shards_of).reshape((-1,) + (1,) * (len(shape) - 1 - position))
    return factor_of


def scatter_about(stream_key, dims, spread, most, cuts=(), dtype=jnp.bfloat16):
    drawn = spread * jax.random.normal(stream_key, dims, jnp.float32)
    if cuts:
        drawn = drawn * steps_of(stream_key, dims, cuts, -0.22, 0.18)
    return jnp.clip(drawn, -most, most).astype(dtype)


def setup_inputs(seed: int = 0) -> dict:
    streams_of = jax.random.split(jax.random.key(seed), 4)
    return {
        "ket_state": scatter_about(streams_of[0], (2, AMPS), 1.0, 6.0, ((1, 1024),), jnp.float32),
        "bra_state": scatter_about(streams_of[1], (2, AMPS), 1.0, 6.0, ((1, 1024),), jnp.float32),
        "gate_matrices": scatter_about(streams_of[2], (LAYERS, GATE, 2 * GATE), (2 * GATE) ** -0.5, 0.5, (), jnp.float32),
    }


highest_precision = lax.Precision.HIGHEST

def layer_bits(layer_index, local_bits):
    first_bits = [local_bits - 6, 0, local_bits // 2 - 3, 1, local_bits - 7]
    ordering = [2, 0, 5, 1, 4, 3]
    first_bit = first_bits[layer_index % 5]
    chosen = [(first_bit + ordering[(slot + layer_index) % 6]) % local_bits for slot in range(6)]
    if layer_index == 0:
        partner_bit = local_bits - 1
    elif layer_index == 1:
        partner_bit = 0
    else:
        partner_bit = (first_bit + 2) % local_bits
    return (chosen, partner_bit)

def block_order(chosen, local_bits):

    def where_bit(qubit):
        return 2 + (local_bits - 1 - qubit)
    gate_axes = [where_bit(chosen[slot]) for slot in reversed(range(len(chosen)))]
    rest_axes = [where_bit(qubit) for qubit in range(local_bits - 1, -1, -1) if qubit not in chosen]
    forward = [1] + rest_axes + [0] + gate_axes
    inverse = [0] * len(forward)
    for place, axis_number in enumerate(forward):
        inverse[axis_number] = place
    return (forward, inverse)

def to_blocks(state, chosen, local_bits, blocks, gate_size):
    forward, inverse = block_order(chosen, local_bits)
    shaped = state.reshape((2, blocks) + (2,) * local_bits)
    return jnp.transpose(shaped, forward).reshape(-1, 2 * gate_size)

def from_blocks(block_state, chosen, local_bits, blocks):
    forward, inverse = block_order(chosen, local_bits)
    shaped = block_state.reshape((blocks,) + (2,) * (local_bits + 1))
    return jnp.transpose(shaped, inverse).reshape(2, -1)

def conj_block(gate_matrix, gate_size):
    real_part = gate_matrix[:, :gate_size]
    imag_part = gate_matrix[:, gate_size:]
    return jnp.concatenate([jnp.concatenate([real_part, -imag_part], 1), jnp.concatenate([imag_part, real_part], 1)], 0)

def outer_grad(bra_blocks, ket_blocks, gate_size):
    product = lax.dot_general(bra_blocks, ket_blocks, (((0,), (0,)), ((), ())), precision=highest_precision, preferred_element_type=jnp.float32)
    real_part = product[:gate_size, :gate_size] + product[gate_size:, gate_size:]
    imag_part = product[:gate_size, gate_size:] - product[gate_size:, :gate_size]
    return jnp.concatenate([real_part, imag_part], 1)

def swap_bits(state, global_bit, partner_bit, total):
    shaped = state.reshape(2, total >> global_bit + 1, 2, 1 << global_bit >> partner_bit + 1, 2, 1 << partner_bit)
    return jnp.swapaxes(shaped, 2, 4).reshape(2, total)

def reference(ket_state, bra_state, gate_matrices):
    amplitudes = AMP_DEV
    gate_size = GATE
    blocks = N_HI * N_LO
    total = amplitudes * blocks
    local_bits = amplitudes.bit_length() - 1
    hi_bits = N_HI.bit_length() - 1
    lo_bits = N_LO.bit_length() - 1
    scale = (gate_size / total) ** 0.5
    results = [None] * LAYERS
    for layer_index in reversed(range(LAYERS)):
        chosen, partner_bit = layer_bits(layer_index, local_bits)
        unapply = conj_block(gate_matrices[layer_index], gate_size)
        ket_blocks = to_blocks(ket_state, chosen, local_bits, blocks, gate_size)
        bra_blocks = to_blocks(bra_state, chosen, local_bits, blocks, gate_size)
        ket_blocks = jnp.dot(ket_blocks, unapply, precision=highest_precision, preferred_element_type=jnp.float32)
        results[layer_index] = outer_grad(bra_blocks, ket_blocks, gate_size) * scale
        bra_blocks = jnp.dot(bra_blocks, unapply, precision=highest_precision, preferred_element_type=jnp.float32)
        ket_state = from_blocks(ket_blocks, chosen, local_bits, blocks)
        bra_state = from_blocks(bra_blocks, chosen, local_bits, blocks)
        if layer_index % 2 == 0:
            global_bit = local_bits + lo_bits + layer_index // 2 % hi_bits
        else:
            global_bit = local_bits + layer_index // 2 % lo_bits
        ket_state = swap_bits(ket_state, global_bit, partner_bit, total)
        bra_state = swap_bits(bra_state, global_bit, partner_bit, total)
    return (ket_state, bra_state, jnp.stack(results))
```

```python
import functools

import jax
import jax.numpy as jnp
from jax import lax
from jax.experimental import pallas as pl
from jax.experimental.pallas import tpu as pltpu
from jax.sharding import PartitionSpec as P

F32 = jnp.float32
BF16 = jnp.bfloat16
MESH = pl.DeviceIdType.MESH
LOCAL_BITS = 14
FIRST = (8, 0, 4, 1, 7)
ORDER = (2, 0, 5, 1, 4, 3)
ROWS = (7, 8, 13, 10, 11, 12, 9)
LANES = (0, 1, 2, 3, 4, 5, 6)
ROWS_MIXED = (7, 8, 13, 4, 5, 6, 9)
NN = (((1,), (0,)), ((), ()))
NT = (((1,), (1,)), ((), ()))
TN = (((0,), (0,)), ((), ()))


def target_bits(layer):
    return [(FIRST[layer] + ORDER[(j + layer) % 6]) % LOCAL_BITS for j in range(6)]


def mm(a, b, dims):
    return lax.dot_general(a, b, dims, preferred_element_type=F32)


def halves(x):
    top = x.astype(BF16)
    return top, (x - top.astype(F32)).astype(BF16)


def mm3(a, b, dims):
    return mm(a[0], b[0], dims) + mm(a[0], b[1], dims) + mm(a[1], b[0], dims)


def gate_code(index, layer, bits):
    code = None
    for j, target in enumerate(target_bits(layer)):
        term = ((index >> bits.index(target)) & 1) << j
        code = term if code is None else code + term
    return code


def rest_position(layer, bits):
    targets = target_bits(layer)
    return [i for i, bit in enumerate(bits) if bit not in targets][0]


def picks(layer, bits):
    row = lax.broadcasted_iota(jnp.int32, (256, 128), 0)
    column = lax.broadcasted_iota(jnp.int32, (256, 128), 1)
    code = gate_code(row & 127, layer, bits) + ((row >> 7) << 6)
    return (code == column).astype(F32).astype(BF16)


def rest_mask(layer, bits):
    i = lax.broadcasted_iota(jnp.int32, (128, 128), 0)
    j = lax.broadcasted_iota(jnp.int32, (128, 128), 1)
    return (((i ^ j) >> rest_position(layer, bits)) & 1) == 0


def spread_gate(u, layer, bits, picked, mask, on_rows):
    row = lax.broadcasted_iota(jnp.int32, (128, 64), 0)
    column = lax.broadcasted_iota(jnp.int32, (128, 64), 1)
    chooser = (gate_code(row, layer, bits) == column).astype(F32).astype(BF16)
    u_parts = halves(u)
    tall = jnp.concatenate([mm(chooser, part, NN).astype(BF16) for part in u_parts], 0)
    out = []
    if on_rows:
        wide = mm(picked, tall, NT)
        for part in range(2):
            columns = slice(128 * part, 128 * part + 128)
            real = jnp.where(mask, wide[:128, columns], 0.0)
            imag = jnp.where(mask, wide[128:, columns], 0.0)
            out.append(jnp.concatenate([jnp.concatenate([real, imag], 1), jnp.concatenate([-imag, real], 1)], 0).astype(BF16))
    else:
        wide = mm(tall, picked, NT)
        for part in range(2):
            rows = slice(128 * part, 128 * part + 128)
            real = jnp.where(mask, wide[rows, :128], 0.0)
            imag = jnp.where(mask, wide[rows, 128:], 0.0)
            out.append(jnp.concatenate([jnp.concatenate([real, -imag], 1), jnp.concatenate([imag, real], 1)], 0).astype(BF16))
    return tuple(out)


def undo_on_rows(gate, x):
    flat = jnp.concatenate([jnp.concatenate([x[0], x[2]], 1), jnp.concatenate([x[1], x[3]], 1)], 0)
    y = mm3(gate, halves(flat), NN)
    return [y[:128, :128], y[128:, :128], y[:128, 128:], y[128:, 128:]]


def undo_on_lanes(gate, x):
    flat = jnp.concatenate([jnp.concatenate([x[0], x[1]], 1), jnp.concatenate([x[2], x[3]], 1)], 0)
    y = mm3(halves(flat), gate, NN)
    return [y[:128, :128], y[:128, 128:], y[128:, :128], y[128:, 128:]]


def outer_on_rows(bra, ket):
    left = jnp.concatenate(bra, 1)
    right = jnp.concatenate([jnp.concatenate([ket[0], ket[1]], 1), jnp.concatenate([ket[1], -ket[0]], 1)], 0)
    return mm3(halves(left), halves(right), NT)


def outer_on_lanes(bra, ket):
    left = jnp.concatenate(bra, 0)
    right = jnp.concatenate([jnp.concatenate([ket[0], ket[1]], 1), jnp.concatenate([ket[1], -ket[0]], 1)], 0)
    return mm3(halves(left), halves(right), TN)


def to_chunks(wide, layer, bits, picked, mask, slot):
    kept = jnp.concatenate([jnp.where(mask, wide[:, :128], 0.0), jnp.where(mask, wide[:, 128:], 0.0)], 1)
    both = mm(jnp.concatenate(halves(kept), 0), picked, NN)
    narrow = jnp.concatenate(halves(both[:128] + both[128:]), 0)
    row = lax.broadcasted_iota(jnp.int32, (256, 256), 0)
    column = lax.broadcasted_iota(jnp.int32, (256, 256), 1)
    code = gate_code(column & 127, layer, bits)
    place = ((code & 15) << 4) + ((code >> 5) << 3) + (((code >> 4) & 1) << 2) + slot
    return mm((row == place).astype(F32).astype(BF16), narrow, NN)


def swap_lane(x, row_bit, lane_bit):
    size, step = 1 << row_bit, 1 << lane_bit
    lane = lax.broadcasted_iota(jnp.int32, (size, 128), 1)
    upper = ((lane >> lane_bit) & 1) == 1
    out = []
    for base in range(0, 128, 2 * size):
        a, b = x[base : base + size], x[base + size : base + 2 * size]
        out.append(jnp.where(upper, pltpu.roll(b, step, 1), a))
        out.append(jnp.where(upper, b, pltpu.roll(a, 128 - step, 1)))
    return jnp.concatenate(out, 0)


def swap_sublane(x, row_bit):
    upper = lax.broadcasted_iota(jnp.int32, (8, 128), 0) >= 4
    tiles = [x[8 * i : 8 * i + 8] for i in range(16)]
    bit = 1 << (row_bit - 3)
    out = [None] * 16
    for i in range(16):
        if not i & bit:
            a, b = tiles[i], tiles[i | bit]
            out[i] = jnp.where(upper, pltpu.roll(b, 4, 0), a)
            out[i | bit] = jnp.where(upper, b, pltpu.roll(a, 4, 0))
    return jnp.concatenate(out, 0)


def kernel(
    scale, ket_ref, bra_ref, gate_ref, ket_out, bra_out, grad_out,
    send_a, recv_a, send_b, recv_b, chunks, partial, packed, column, final,
    a_send, a_recv, b_send, b_recv, c_send, c_recv, z_send, z_recv, f_send, f_recv, near, far,
):
    hi, lo = lax.axis_index("hi"), lax.axis_index("lo")
    z, y = lo & 31, lo >> 5

    def ring(step):
        return (hi, (lo & 32) + ((z + step) & 31))

    barrier = pltpu.get_barrier_semaphore()

    def greet(device):
        pl.semaphore_signal(barrier, inc=1, device_id=device, device_id_type=MESH)

    greet((hi ^ 4, lo ^ 2))
    for k in (1, 2, 3):
        greet((hi ^ k, lo ^ 1))
    for step in (1, 2, 3, 4):
        greet(ring(step))
        greet(ring(-step))

    me = hi * 2 + y

    def greet_plane(k, carry):
        other = me ^ k
        greet((other >> 1, (other & 1) * 32 + z))
        return carry

    lax.fori_loop(1, 32, greet_plane, 0)

    def layer_setup(layer, bits, on_rows):
        picked, mask = picks(layer, bits), rest_mask(layer, bits)
        return picked, mask, spread_gate(gate_ref[layer], layer, bits, picked, mask, on_rows)

    pick4, mask4, gate4 = layer_setup(4, ROWS, True)
    pick3, mask3, gate3 = layer_setup(3, LANES, False)

    x5 = [swap_sublane(r[i], 6) for r in (ket_ref, bra_ref) for i in range(2)]
    x4 = undo_on_rows(gate4, x5)
    x3 = undo_on_lanes(gate3, x4)
    mine = ((hi >> 2) & 1) * 2 + ((lo >> 1) & 1)
    for i in range(4):
        ready = swap_lane(x3[i], 5, 3)
        for block in range(4):
            send_a[block, i] = ready[32 * block : 32 * block + 32]
    recv_a[mine] = send_a[mine]

    pl.semaphore_wait(barrier, 43)

    copies_a = []
    for d in (3, 1, 2):
        copy = pltpu.make_async_remote_copy(
            send_a.at[mine ^ d], recv_a.at[mine], a_send.at[d], a_recv.at[d],
            device_id=(hi ^ (4 if d & 2 else 0), lo ^ (2 if d & 1 else 0)), device_id_type=MESH,
        )
        copy.start()
        copies_a.append(copy)
    for step in (4, -4):
        pl.semaphore_signal(near, inc=1, device_id=ring(step), device_id_type=MESH)

    def plane_copy(batch, k):
        other = me ^ k
        return pltpu.make_async_remote_copy(
            chunks.at[batch, other], partial.at[batch, me], c_send.at[batch, k], c_recv.at[batch, k],
            device_id=(other >> 1, (other & 1) * 32 + z), device_id_type=MESH,
        )

    def send_plane(batch, value):
        chunks[batch] = value.reshape(32, 8, 128)
        partial[batch, me] = chunks[batch, me]

        def go(k, carry):
            plane_copy(batch, k).start()
            return carry

        lax.fori_loop(1, 32, go, 0)

    def wait_plane(batch):
        def go(k, carry):
            plane_copy(batch, k).wait()
            return carry

        lax.fori_loop(1, 32, go, 0)
        return jnp.sum(partial[batch], 0)

    first = to_chunks(outer_on_rows(x5[2:], x4[:2]), 4, ROWS, pick4, mask4, 0)
    first += to_chunks(outer_on_lanes(x4[2:], x3[:2]), 3, LANES, pick3, mask3, 3)
    send_plane(0, first)

    pick2, mask2, gate2 = layer_setup(2, ROWS_MIXED, True)
    pick1, mask1, gate1 = layer_setup(1, LANES, False)
    pick0, mask0, gate0 = layer_setup(0, ROWS, True)
    pl.semaphore_wait(near, 2)
    for step in (8, -8):
        pl.semaphore_signal(far, inc=1, device_id=ring(step), device_id_type=MESH)

    for copy in copies_a:
        copy.wait()
    x = [jnp.concatenate([recv_a[block, i] for block in range(4)], 0) for i in range(4)]
    x = [swap_lane(v, 5, 3) for v in x]
    mixed = [swap_lane(swap_lane(swap_lane(v, 3, 4), 4, 5), 5, 6) for v in x]
    x2 = undo_on_rows(gate2, mixed)
    turned = [swap_lane(swap_lane(swap_lane(v, 3, 4), 4, 5), 5, 6) for v in x2]
    x1 = undo_on_lanes(gate1, turned)
    x0 = undo_on_rows(gate0, x1)

    second = to_chunks(outer_on_rows(x1[2:], x0[:2]), 0, ROWS, pick0, mask0, 0)
    second += to_chunks(outer_on_lanes(turned[2:], x1[:2]), 1, LANES, pick1, mask1, 1)
    second += to_chunks(outer_on_rows(mixed[2:], x2[:2]), 2, ROWS_MIXED, pick2, mask2, 2)
    send_plane(1, second)

    own = ((hi >> 1) & 1) * 4 + (lo & 1) * 2 + (hi & 1)
    for i in range(4):
        ready = swap_sublane(swap_lane(swap_lane(x0[i], 5, 6), 4, 0), 3)
        for block in range(8):
            for top in range(2):
                send_b[block, i, top] = ready[64 * top + 8 * block : 64 * top + 8 * block + 8]
    recv_b[own] = send_b[own]
    copies_b = []
    for d in range(1, 8):
        copy = pltpu.make_async_remote_copy(
            send_b.at[own ^ d], recv_b.at[own], b_send.at[d], b_recv.at[d],
            device_id=(hi ^ ((2 if d & 4 else 0) + (d & 1)), lo ^ (1 if d & 2 else 0)), device_id_type=MESH,
        )
        copy.start()
        copies_b.append(copy)

    sum1 = wait_plane(0)
    sum2 = wait_plane(1)
    sub = lax.broadcasted_iota(jnp.int32, (8, 128), 0)
    for q in range(2):
        late, early = (pltpu.roll(sum2, 4, 0), pltpu.roll(sum1, 4, 0)) if q else (sum2, sum1)
        other = sum1 if q else pltpu.roll(sum1, 4, 0)
        packed[q] = jnp.where(sub < 3, late, jnp.where(sub == 3, early, other))
    pl.semaphore_wait(far, 2)

    def column_copy(q):
        return pltpu.make_async_remote_copy(
            packed.at[q], column.at[z], z_send.at[q], z_recv.at[z],
            device_id=(hi, (lo & 32) + hi + 16 * q), device_id_type=MESH,
        )

    for q in range(2):
        @pl.when(z != hi + 16 * q)
        def _():
            column_copy(q).start()

        @pl.when(z == hi + 16 * q)
        def _():
            column[z] = packed[q]

    for copy in copies_b:
        copy.wait()
    for i in range(4):
        v = jnp.concatenate([recv_b[block, i, top] for top in range(2) for block in range(8)], 0)
        v = swap_lane(swap_lane(swap_sublane(v, 3), 4, 0), 5, 6)
        (ket_out, bra_out)[i // 2][i % 2] = swap_sublane(v, 6)

    for q in range(2):
        @pl.when(z != hi + 16 * q)
        def _():
            column_copy(q).wait_send()

    owner = (z & 15) == hi

    def final_copy(k, slot):
        return pltpu.make_async_remote_copy(
            final, final, f_send.at[k], f_recv, device_id=(hi ^ k, lo), device_id_type=MESH,
        )

    @pl.when(owner)
    def _():
        def arrive(source, carry):
            @pl.when(source != z)
            def _():
                pltpu.make_async_remote_copy(
                    packed.at[0], column.at[source], z_send.at[0], z_recv.at[source],
                    device_id=(hi, lo), device_id_type=MESH,
                ).wait_recv()

            return carry

        lax.fori_loop(0, 32, arrive, 0)
        final[...] = jnp.sum(column[...], 0) * scale

        def give(k, carry):
            final_copy(k, 0).start()
            return carry

        def given(k, carry):
            final_copy(k, 0).wait_send()
            return carry

        lax.fori_loop(1, 16, give, 0)
        lax.fori_loop(1, 16, given, 0)

    @pl.when(jnp.logical_not(owner))
    def _():
        final_copy(0, 0).wait_recv()

    grad_out[...] = final[...]


def body(ket_state, bra_state, gate_matrices):
    scale = (64 / (16384 * lax.axis_size("hi") * lax.axis_size("lo"))) ** 0.5
    vmem = pl.BlockSpec(memory_space=pltpu.VMEM)
    state = jax.ShapeDtypeStruct((2, 128, 128), F32)
    dma = pltpu.SemaphoreType.DMA
    ket, bra, grad = pl.pallas_call(
        functools.partial(kernel, scale),
        out_shape=(state, state, jax.ShapeDtypeStruct((8, 128), F32)),
        in_specs=[vmem] * 3,
        out_specs=(vmem,) * 3,
        scratch_shapes=[
            pltpu.VMEM((4, 4, 32, 128), F32),
            pltpu.VMEM((4, 4, 32, 128), F32),
            pltpu.VMEM((8, 4, 2, 8, 128), F32),
            pltpu.VMEM((8, 4, 2, 8, 128), F32),
            pltpu.VMEM((2, 32, 8, 128), F32),
            pltpu.VMEM((2, 32, 8, 128), F32),
            pltpu.VMEM((2, 8, 128), F32),
            pltpu.VMEM((32, 8, 128), F32),
            pltpu.VMEM((8, 128), F32),
            dma((4,)), dma((4,)), dma((8,)), dma((8,)),
            dma((2, 32)), dma((2, 32)), dma((2,)), dma((32,)), dma((16,)), dma,
            pltpu.SemaphoreType.REGULAR, pltpu.SemaphoreType.REGULAR,
        ],
        compiler_params=pltpu.CompilerParams(collective_id=0, has_side_effects=True, vmem_limit_bytes=40 * 2**20),
        name="window",
    )(ket_state.reshape(2, 128, 128), bra_state.reshape(2, 128, 128), gate_matrices)
    amplitudes = ket_state.shape[1]
    return ket.reshape(2, amplitudes), bra.reshape(2, amplitudes), grad[:5].reshape(5, 1, 128)


def solution(mesh):
    placed = (P(None, ("hi", "lo")), P(None, ("hi", "lo")), P())
    return jax.shard_map(
        body,
        mesh=mesh,
        in_specs=placed,
        out_specs=(P(None, ("hi", "lo")), P(None, ("hi", "lo")), P(None, "lo", None)),
        check_vma=False,
    )
```

```python
import functools

import jax
import jax.numpy as jnp
from jax import lax
from jax.experimental import pallas as pl
from jax.experimental.pallas import tpu as pltpu
from jax.sharding import PartitionSpec as P

F32 = jnp.float32
BF16 = jnp.bfloat16
MESH = pl.DeviceIdType.MESH
LOCAL_BITS = 14
FIRST = (8, 0, 4, 1, 7)
ORDER = (2, 0, 5, 1, 4, 3)
ROWS = (7, 8, 13, 10, 11, 12, 9)
LANES = (0, 1, 2, 3, 4, 5, 6)
ROWS_MIXED = (7, 8, 13, 4, 5, 6, 9)
NN = (((1,), (0,)), ((), ()))
NT = (((1,), (1,)), ((), ()))
TN = (((0,), (0,)), ((), ()))


def target_bits(layer):
    return [(FIRST[layer] + ORDER[(j + layer) % 6]) % LOCAL_BITS for j in range(6)]


def mm(a, b, dims):
    return lax.dot_general(a, b, dims, preferred_element_type=F32)


def halves(x):
    top = x.astype(BF16)
    return top, (x - top.astype(F32)).astype(BF16)


def mm3(a, b, dims):
    return mm(a[0], b[0], dims) + mm(a[0], b[1], dims) + mm(a[1], b[0], dims)


def gate_code(index, layer, bits):
    code = None
    for j, target in enumerate(target_bits(layer)):
        term = ((index >> bits.index(target)) & 1) << j
        code = term if code is None else code + term
    return code


def rest_position(layer, bits):
    targets = target_bits(layer)
    return [i for i, bit in enumerate(bits) if bit not in targets][0]


def picks(layer, bits):
    row = lax.broadcasted_iota(jnp.int32, (256, 128), 0)
    column = lax.broadcasted_iota(jnp.int32, (256, 128), 1)
    code = gate_code(row & 127, layer, bits) + ((row >> 7) << 6)
    return (code == column).astype(F32).astype(BF16)


def rest_mask(layer, bits):
    i = lax.broadcasted_iota(jnp.int32, (128, 128), 0)
    j = lax.broadcasted_iota(jnp.int32, (128, 128), 1)
    return (((i ^ j) >> rest_position(layer, bits)) & 1) == 0


def spread_gate(u, layer, bits, picked, mask, on_rows):
    row = lax.broadcasted_iota(jnp.int32, (128, 64), 0)
    column = lax.broadcasted_iota(jnp.int32, (128, 64), 1)
    chooser = (gate_code(row, layer, bits) == column).astype(F32).astype(BF16)
    u_parts = halves(u)
    tall = jnp.concatenate([mm(chooser, part, NN).astype(BF16) for part in u_parts], 0)
    out = []
    if on_rows:
        wide = mm(picked, tall, NT)
        for part in range(2):
            columns = slice(128 * part, 128 * part + 128)
            real = jnp.where(mask, wide[:128, columns], 0.0)
            imag = jnp.where(mask, wide[128:, columns], 0.0)
            out.append(jnp.concatenate([jnp.concatenate([real, imag], 1), jnp.concatenate([-imag, real], 1)], 0).astype(BF16))
    else:
        wide = mm(tall, picked, NT)
        for part in range(2):
            rows = slice(128 * part, 128 * part + 128)
            real = jnp.where(mask, wide[rows, :128], 0.0)
            imag = jnp.where(mask, wide[rows, 128:], 0.0)
            out.append(jnp.concatenate([jnp.concatenate([real, -imag], 1), jnp.concatenate([imag, real], 1)], 0).astype(BF16))
    return tuple(out)


def undo_on_rows(gate, x):
    flat = jnp.concatenate([jnp.concatenate([x[0], x[2]], 1), jnp.concatenate([x[1], x[3]], 1)], 0)
    y = mm3(gate, halves(flat), NN)
    return [y[:128, :128], y[128:, :128], y[:128, 128:], y[128:, 128:]]


def undo_on_lanes(gate, x):
    flat = jnp.concatenate([jnp.concatenate([x[0], x[1]], 1), jnp.concatenate([x[2], x[3]], 1)], 0)
    y = mm3(halves(flat), gate, NN)
    return [y[:128, :128], y[:128, 128:], y[128:, :128], y[128:, 128:]]


def outer_on_rows(bra, ket):
    left = jnp.concatenate(bra, 1)
    right = jnp.concatenate([jnp.concatenate([ket[0], ket[1]], 1), jnp.concatenate([ket[1], -ket[0]], 1)], 0)
    return mm3(halves(left), halves(right), NT)


def outer_on_lanes(bra, ket):
    left = jnp.concatenate(bra, 0)
    right = jnp.concatenate([jnp.concatenate([ket[0], ket[1]], 1), jnp.concatenate([ket[1], -ket[0]], 1)], 0)
    return mm3(halves(left), halves(right), TN)


def to_chunks(wide, layer, bits, picked, mask, slot, by_plane):
    kept = jnp.concatenate([jnp.where(mask, wide[:, :128], 0.0), jnp.where(mask, wide[:, 128:], 0.0)], 1)
    both = mm(jnp.concatenate(halves(kept), 0), picked, NN)
    narrow = jnp.concatenate(halves(both[:128] + both[128:]), 0)
    shape = (256 if by_plane else 64, 256)
    row = lax.broadcasted_iota(jnp.int32, shape, 0)
    column = lax.broadcasted_iota(jnp.int32, shape, 1)
    code = gate_code(column & 127, layer, bits)
    if by_plane:
        place = (((code & 15) ^ 1) << 4) + ((code >> 5) << 3) + (((code >> 4) & 1) << 2) + slot
    else:
        place = (((code & 7) ^ 1) << 3) + (code >> 3)
    return mm((row == place).astype(F32).astype(BF16), narrow, NN)


def swap_lane(x, row_bit, lane_bit):
    size, step = 1 << row_bit, 1 << lane_bit
    lane = lax.broadcasted_iota(jnp.int32, (size, 128), 1)
    upper = ((lane >> lane_bit) & 1) == 1
    out = []
    for base in range(0, 128, 2 * size):
        a, b = x[base : base + size], x[base + size : base + 2 * size]
        out.append(jnp.where(upper, pltpu.roll(b, step, 1), a))
        out.append(jnp.where(upper, b, pltpu.roll(a, 128 - step, 1)))
    return jnp.concatenate(out, 0)


def swap_sublane(x, row_bit):
    upper = lax.broadcasted_iota(jnp.int32, (8, 128), 0) >= 4
    tiles = [x[8 * i : 8 * i + 8] for i in range(16)]
    bit = 1 << (row_bit - 3)
    out = [None] * 16
    for i in range(16):
        if not i & bit:
            a, b = tiles[i], tiles[i | bit]
            out[i] = jnp.where(upper, pltpu.roll(b, 4, 0), a)
            out[i | bit] = jnp.where(upper, b, pltpu.roll(a, 4, 0))
    return jnp.concatenate(out, 0)


def hops(k):
    in_y = 1 if k & 1 else (2 if k & 16 else 0)
    in_x = 1 if k & 4 else (2 if k & 8 else 0)
    return 2 * (in_x + in_y) + ((k >> 1) & 1)


IN_PLANE = sorted(range(1, 32), key=hops, reverse=True)
IN_LINE = [k >> 1 for k in IN_PLANE if k < 16 and not k & 1]


def kernel(
    scale, ket_ref, bra_ref, gate_hbm, outs,
    states, gates, send_a, recv_a, send_b, recv_b, chunks, partial, packed, column,
    line_out, line_in, rows_out, rows_in, extra, share, final,
    in_sem, a_send, a_recv, b_send, b_recv, c_send, c_recv, z_send, z_recv, l_send, l_recv, q_send, q_recv, f_send, f_recv, line, near, mid, far,
):
    hi, lo = lax.axis_index("hi"), lax.axis_index("lo")
    z, y = lo & 31, lo >> 5
    me = hi * 2 + y
    loads = [
        pltpu.make_async_copy(gate_hbm, gates, in_sem.at[2]),
        pltpu.make_async_copy(ket_ref, states.at[0], in_sem.at[0]),
        pltpu.make_async_copy(bra_ref, states.at[1], in_sem.at[1]),
    ]
    for load in loads:
        load.start()

    def ring(step):
        return (hi, (lo & 32) + ((z + step) & 31))

    def in_plane(k):
        return (hi ^ (k >> 1), lo ^ ((k & 1) * 32))

    barrier = pltpu.get_barrier_semaphore()

    def greet(device):
        pl.semaphore_signal(barrier, inc=1, device_id=device, device_id_type=MESH)

    for step in (2, -2, 1, -1):
        greet(ring(step))
    for k in IN_LINE:
        greet((hi ^ k, lo))
    for k in (16, 17, 1):
        greet(in_plane(k))
    extra[...] = jnp.zeros((2, 8, 128), F32)
    loads[0].wait()

    def layer_setup(layer, bits, on_rows):
        picked, mask = picks(layer, bits), rest_mask(layer, bits)
        return picked, mask, spread_gate(gates[layer], layer, bits, picked, mask, on_rows)

    pick4, mask4, gate4 = layer_setup(4, ROWS, True)
    pick3, mask3, gate3 = layer_setup(3, LANES, False)

    loads[1].wait()
    loads[2].wait()
    x5 = [swap_sublane(states[s, pl.ds(c, 128, stride=2), :], 6) for s in range(2) for c in range(2)]
    x4 = undo_on_rows(gate4, x5)
    x3 = undo_on_lanes(gate3, x4)
    mine = ((hi >> 2) & 1) * 2 + ((lo >> 1) & 1)
    for i in range(4):
        ready = swap_lane(x3[i], 5, 3)
        for block in range(4):
            send_a[block, i] = ready[32 * block : 32 * block + 32]

    pl.semaphore_wait(barrier, 14)

    def copy_a(d):
        return pltpu.make_async_remote_copy(
            send_a.at[mine ^ d], recv_a.at[mine], a_send.at[d], a_recv.at[d],
            device_id=(hi ^ (4 if d & 2 else 0), lo ^ (2 if d & 1 else 0)), device_id_type=MESH,
        )

    copy_a(1).start()
    copy_a(2).start()
    for k in IN_LINE:
        pl.semaphore_signal(line, inc=1, device_id=(hi ^ k, lo), device_id_type=MESH)
    for step in (2, -2):
        pl.semaphore_signal(near, inc=1, device_id=ring(step), device_id_type=MESH)
    recv_a[mine] = send_a[mine]

    def all_of(ref, sem):
        pltpu.make_async_copy(ref, ref, sem).wait()

    first = to_chunks(outer_on_rows(x5[2:], x4[:2]), 4, ROWS, pick4, mask4, 0, True)
    first += to_chunks(outer_on_lanes(x4[2:], x3[:2]), 3, LANES, pick3, mask3, 3, True)
    chunks[...] = first.reshape(32, 8, 128)
    partial[me] = chunks[me]
    pl.semaphore_wait(line, 7)
    copy_a(3).start()
    pl.semaphore_wait(near, 2)
    for step in (4, -4):
        pl.semaphore_signal(mid, inc=1, device_id=ring(step), device_id_type=MESH)
    for k in IN_PLANE:
        pltpu.make_async_remote_copy(
            chunks.at[me ^ k], partial.at[me], c_send, c_recv, device_id=in_plane(k), device_id_type=MESH,
        ).start()

    pick2, mask2, gate2 = layer_setup(2, ROWS_MIXED, True)
    pick1, mask1, gate1 = layer_setup(1, LANES, False)
    pick0, mask0, gate0 = layer_setup(0, ROWS, True)
    pl.semaphore_wait(mid, 2)
    for step in (8, -8):
        pl.semaphore_signal(far, inc=1, device_id=ring(step), device_id_type=MESH)

    for d in (1, 2, 3):
        copy_a(d).wait()
    x = [jnp.concatenate([recv_a[block, i] for block in range(4)], 0) for i in range(4)]
    x = [swap_lane(v, 5, 3) for v in x]
    mixed = [swap_lane(swap_lane(swap_lane(v, 3, 4), 4, 5), 5, 6) for v in x]

    def send_line(layer, value):
        line_out[layer] = value.reshape(8, 8, 128)
        for k in IN_LINE:
            pltpu.make_async_remote_copy(
                line_out.at[layer, (hi & 7) ^ k], line_in.at[layer, hi & 7], l_send.at[layer], l_recv.at[layer],
                device_id=(hi ^ k, lo), device_id_type=MESH,
            ).start()
        line_in[layer, hi & 7] = line_out[layer, hi & 7]

    x2 = undo_on_rows(gate2, mixed)
    turned = [swap_lane(swap_lane(swap_lane(v, 3, 4), 4, 5), 5, 6) for v in x2]
    x1 = undo_on_lanes(gate1, turned)
    send_line(2, to_chunks(outer_on_rows(mixed[2:], x2[:2]), 2, ROWS_MIXED, pick2, mask2, 0, False))
    x0 = undo_on_rows(gate0, x1)
    send_line(1, to_chunks(outer_on_lanes(turned[2:], x1[:2]), 1, LANES, pick1, mask1, 0, False))
    send_line(0, to_chunks(outer_on_rows(x1[2:], x0[:2]), 0, ROWS, pick0, mask0, 0, False))

    own = ((hi >> 1) & 1) * 4 + (lo & 1) * 2 + (hi & 1)
    for i in range(4):
        ready = swap_sublane(swap_lane(swap_lane(x0[i], 5, 6), 4, 0), 3)
        for block in range(8):
            for top in range(2):
                send_b[block, i, top] = ready[64 * top + 8 * block : 64 * top + 8 * block + 8]
    recv_b[own] = send_b[own]
    copies_b = []
    for d in range(1, 8):
        copy = pltpu.make_async_remote_copy(
            send_b.at[own ^ d], recv_b.at[own], b_send.at[d], b_recv.at[d],
            device_id=(hi ^ ((2 if d & 4 else 0) + (d & 1)), lo ^ (1 if d & 2 else 0)), device_id_type=MESH,
        )
        copy.start()
        copies_b.append(copy)

    sub = lax.broadcasted_iota(jnp.int32, (8, 128), 0)
    all_of(partial.at[pl.ds(0, 31)], c_recv)
    sum1 = jnp.sum(partial[...], 0)
    turned1 = pltpu.roll(sum1, 4, 0)
    for q in range(2):
        three, four = (turned1, sum1) if q else (sum1, turned1)
        packed[q] = jnp.where(sub == 3, three, jnp.where(sub == 4, four, 0.0))
    pl.semaphore_wait(far, 2)

    def column_copy(q):
        return pltpu.make_async_remote_copy(
            packed.at[q], column.at[z], z_send.at[q], z_recv,
            device_id=(hi, (lo & 32) + (hi ^ 1) + 16 * q), device_id_type=MESH,
        )

    sums = []
    for layer in (2, 1, 0):
        all_of(line_in.at[layer, pl.ds(0, 7)], l_recv.at[layer])
        sums.insert(0, jnp.sum(line_in[layer], 0))
    for q in range(4):
        value = jnp.zeros((8, 128), F32)
        for layer in range(3):
            shift = (layer - q) % 8
            value = jnp.where(sub & 3 == layer, pltpu.roll(sums[layer], shift, 0) if shift else sums[layer], value)
        rows_out[q] = value

    def row_copy(q):
        return pltpu.make_async_remote_copy(
            rows_out.at[q], rows_in.at[z], q_send.at[q], q_recv,
            device_id=(hi, (lo & 32) + ((hi & 7) ^ 1) + 8 * q), device_id_type=MESH,
        )

    for q in range(4):
        @pl.when(z != ((hi & 7) ^ 1) + 8 * q)
        def _():
            row_copy(q).start()

        @pl.when(z == ((hi & 7) ^ 1) + 8 * q)
        def _():
            rows_in[z] = rows_out[q]

    for q in range(2):
        @pl.when(z != (hi ^ 1) + 16 * q)
        def _():
            column_copy(q).start()

        @pl.when(z == (hi ^ 1) + 16 * q)
        def _():
            column[z] = packed[q]

    for copy in copies_b:
        copy.wait()
    for i in range(4):
        v = jnp.concatenate([recv_b[block, i, top] for top in range(2) for block in range(8)], 0)
        v = swap_lane(swap_lane(swap_sublane(v, 3), 4, 0), 5, 6)
        outs[pl.ds(256 * (i // 2) + i % 2, 128, stride=2), :] = swap_sublane(v, 6)
    all_of(chunks.at[pl.ds(0, 31)], c_send)
    for layer in range(3):
        all_of(line_out.at[layer, pl.ds(0, 7)], l_send.at[layer])
    for q in range(2):
        @pl.when(z != (hi ^ 1) + 16 * q)
        def _():
            column_copy(q).wait_send()

    for q in range(4):
        @pl.when(z != ((hi & 7) ^ 1) + 8 * q)
        def _():
            row_copy(q).wait_send()

    sink = ((z ^ hi) & 7) == 1
    slot = (hi >> 3) * 2 + y

    @pl.when(z & 15 == (hi ^ 1))
    def _():
        all_of(column.at[pl.ds(0, 31)], z_recv)
        extra[y] = jnp.sum(column[...], 0)

    @pl.when(sink)
    def _():
        all_of(rows_in.at[pl.ds(0, 31)], q_recv)
        total = jnp.sum(rows_in[...], 0)
        share[0] = jnp.where(sub < 3, total, 0.0) + extra[0]
        share[1] = jnp.where(sub < 3, pltpu.roll(total, 4, 0), 0.0) + extra[1]
        for k in IN_PLANE:
            pltpu.make_async_remote_copy(
                share.at[y ^ (k & 1)], final.at[slot], f_send, f_recv, device_id=in_plane(k), device_id_type=MESH,
            ).start()
        final[slot] = share[y]
        all_of(final.at[pl.ds(0, 3)], f_recv)

    @pl.when(jnp.logical_not(sink))
    def _():
        all_of(final.at[pl.ds(0, 4)], f_recv)

    outs[512:520, :] = jnp.sum(final[...], 0) * scale
    @pl.when(sink)
    def _():
        all_of(column.at[pl.ds(0, 31)], f_send)


def body(ket_state, bra_state, gate_matrices):
    scale = (64 / (16384 * lax.axis_size("hi") * lax.axis_size("lo"))) ** 0.5
    amplitudes = ket_state.shape[1]
    hbm = pl.BlockSpec(memory_space=pltpu.HBM)
    dma = pltpu.SemaphoreType.DMA
    regular = pltpu.SemaphoreType.REGULAR
    whole = pl.pallas_call(
        functools.partial(kernel, scale),
        out_shape=jax.ShapeDtypeStruct((520, 128), F32),
        in_specs=[hbm] * 3,
        out_specs=pl.BlockSpec(memory_space=pltpu.VMEM),
        scratch_shapes=[
            pltpu.VMEM((2, 256, 128), F32),
            pltpu.VMEM((5, 64, 128), F32),
            pltpu.VMEM((4, 4, 32, 128), F32),
            pltpu.VMEM((4, 4, 32, 128), F32),
            pltpu.VMEM((8, 4, 2, 8, 128), F32),
            pltpu.VMEM((8, 4, 2, 8, 128), F32),
            pltpu.VMEM((32, 8, 128), F32),
            pltpu.VMEM((32, 8, 128), F32),
            pltpu.VMEM((2, 8, 128), F32),
            pltpu.VMEM((32, 8, 128), F32),
            pltpu.VMEM((3, 8, 8, 128), F32),
            pltpu.VMEM((3, 8, 8, 128), F32),
            pltpu.VMEM((4, 8, 128), F32),
            pltpu.VMEM((32, 8, 128), F32),
            pltpu.VMEM((2, 8, 128), F32),
            pltpu.VMEM((2, 8, 128), F32),
            pltpu.VMEM((4, 8, 128), F32),
            dma((3,)), dma((4,)), dma((4,)), dma((8,)), dma((8,)),
            dma, dma, dma((2,)), dma, dma((3,)), dma((3,)), dma((4,)), dma, dma, dma,
            regular, regular, regular, regular,
        ],
        compiler_params=pltpu.CompilerParams(collective_id=0, has_side_effects=True, vmem_limit_bytes=40 * 2**20),
        name="window",
    )(
        *(
            pltpu.with_memory_space_constraint(v, pltpu.HBM)
            for v in (
                ket_state.reshape(2, 128, 128).transpose(1, 0, 2).reshape(256, 128),
                bra_state.reshape(2, 128, 128).transpose(1, 0, 2).reshape(256, 128),
                gate_matrices,
            )
        ),
    )
    ket, bra = (v.reshape(128, 2, 128).transpose(1, 0, 2).reshape(2, amplitudes) for v in (whole[:256], whole[256:512]))
    return ket, bra, whole[512:517].reshape(5, 1, 128)


def solution(mesh):
    placed = (P(None, ("hi", "lo")), P(None, ("hi", "lo")), P())
    return jax.shard_map(
        body,
        mesh=mesh,
        in_specs=placed,
        out_specs=(P(None, ("hi", "lo")), P(None, ("hi", "lo")), P(None, "lo", None)),
        check_vma=False,
    )
```

```python
import functools

import jax
import jax.numpy as jnp
from jax import lax
from jax.experimental import pallas as pl
from jax.experimental.pallas import tpu as pltpu
from jax.sharding import PartitionSpec as P

F32 = jnp.float32
BF16 = jnp.bfloat16
MESH = pl.DeviceIdType.MESH
LOCAL_BITS = 14
FIRST = (8, 0, 4, 1, 7)
ORDER = (2, 0, 5, 1, 4, 3)
ROWS = (7, 8, 13, 10, 11, 12, 9)
LANES = (0, 1, 2, 3, 4, 5, 6)
ROWS_MIXED = (7, 8, 13, 4, 5, 6, 9)
NN = (((1,), (0,)), ((), ()))
NT = (((1,), (1,)), ((), ()))
TN = (((0,), (0,)), ((), ()))


def target_bits(layer):
    return [(FIRST[layer] + ORDER[(j + layer) % 6]) % LOCAL_BITS for j in range(6)]


def mm(a, b, dims):
    return lax.dot_general(a, b, dims, preferred_element_type=F32)


def halves(x):
    top = x.astype(BF16)
    return top, (x - top.astype(F32)).astype(BF16)


def mm3(a, b, dims):
    return mm(a[0], b[0], dims) + mm(a[0], b[1], dims) + mm(a[1], b[0], dims)


def gate_code(index, layer, bits):
    code = None
    for j, target in enumerate(target_bits(layer)):
        term = ((index >> bits.index(target)) & 1) << j
        code = term if code is None else code + term
    return code


def rest_position(layer, bits):
    targets = target_bits(layer)
    return [i for i, bit in enumerate(bits) if bit not in targets][0]


def holder(z):
    return ((z & 3) << 1) + 1 - (z >> 2)


def picks(layer, bits):
    row = lax.broadcasted_iota(jnp.int32, (256, 128), 0)
    column = lax.broadcasted_iota(jnp.int32, (256, 128), 1)
    code = gate_code(row & 127, layer, bits) + ((row >> 7) << 6)
    return (code == column).astype(F32).astype(BF16)


def rest_mask(layer, bits):
    i = lax.broadcasted_iota(jnp.int32, (128, 128), 0)
    j = lax.broadcasted_iota(jnp.int32, (128, 128), 1)
    return (((i ^ j) >> rest_position(layer, bits)) & 1) == 0


def spread_gate(u, layer, bits, picked, mask, on_rows):
    row = lax.broadcasted_iota(jnp.int32, (128, 64), 0)
    column = lax.broadcasted_iota(jnp.int32, (128, 64), 1)
    chooser = (gate_code(row, layer, bits) == column).astype(F32).astype(BF16)
    u_parts = halves(u)
    tall = jnp.concatenate([mm(chooser, part, NN).astype(BF16) for part in u_parts], 0)
    out = []
    if on_rows:
        wide = mm(picked, tall, NT)
        for part in range(2):
            columns = slice(128 * part, 128 * part + 128)
            real = jnp.where(mask, wide[:128, columns], 0.0)
            imag = jnp.where(mask, wide[128:, columns], 0.0)
            out.append(jnp.concatenate([jnp.concatenate([real, imag], 1), jnp.concatenate([-imag, real], 1)], 0).astype(BF16))
    else:
        wide = mm(tall, picked, NT)
        for part in range(2):
            rows = slice(128 * part, 128 * part + 128)
            real = jnp.where(mask, wide[rows, :128], 0.0)
            imag = jnp.where(mask, wide[rows, 128:], 0.0)
            out.append(jnp.concatenate([jnp.concatenate([real, -imag], 1), jnp.concatenate([imag, real], 1)], 0).astype(BF16))
    return tuple(out)


def undo_on_rows(gate, x):
    flat = jnp.concatenate([jnp.concatenate([x[0], x[2]], 1), jnp.concatenate([x[1], x[3]], 1)], 0)
    y = mm3(gate, halves(flat), NN)
    return [y[:128, :128], y[128:, :128], y[:128, 128:], y[128:, 128:]]


def undo_on_lanes(gate, x):
    flat = jnp.concatenate([jnp.concatenate([x[0], x[1]], 1), jnp.concatenate([x[2], x[3]], 1)], 0)
    y = mm3(halves(flat), gate, NN)
    return [y[:128, :128], y[:128, 128:], y[128:, :128], y[128:, 128:]]


def outer_on_rows(bra, ket):
    left = jnp.concatenate(bra, 1)
    right = jnp.concatenate([jnp.concatenate([ket[0], ket[1]], 1), jnp.concatenate([ket[1], -ket[0]], 1)], 0)
    return mm3(halves(left), halves(right), NT)


def outer_on_lanes(bra, ket):
    left = jnp.concatenate(bra, 0)
    right = jnp.concatenate([jnp.concatenate([ket[0], ket[1]], 1), jnp.concatenate([ket[1], -ket[0]], 1)], 0)
    return mm3(halves(left), halves(right), TN)


def to_chunks(wide, layer, bits, picked, mask, slot, by_plane):
    kept = jnp.concatenate([jnp.where(mask, wide[:, :128], 0.0), jnp.where(mask, wide[:, 128:], 0.0)], 1)
    both = mm(jnp.concatenate(halves(kept), 0), picked, NN)
    narrow = jnp.concatenate(halves(both[:128] + both[128:]), 0)
    shape = (256 if by_plane else 64, 256)
    row = lax.broadcasted_iota(jnp.int32, shape, 0)
    column = lax.broadcasted_iota(jnp.int32, shape, 1)
    code = gate_code(column & 127, layer, bits)
    if by_plane:
        place = (((code & 8) + holder(code & 7)) << 4) + ((code >> 5) << 3) + (((code >> 4) & 1) << 2) + slot
    else:
        place = (holder(code & 7) << 3) + (code >> 3)
    return mm((row == place).astype(F32).astype(BF16), narrow, NN)


def swap_lane(x, row_bit, lane_bit):
    size, step = 1 << row_bit, 1 << lane_bit
    lane = lax.broadcasted_iota(jnp.int32, (size, 128), 1)
    upper = ((lane >> lane_bit) & 1) == 1
    out = []
    for base in range(0, 128, 2 * size):
        a, b = x[base : base + size], x[base + size : base + 2 * size]
        out.append(jnp.where(upper, pltpu.roll(b, step, 1), a))
        out.append(jnp.where(upper, b, pltpu.roll(a, 128 - step, 1)))
    return jnp.concatenate(out, 0)


def swap_sublane(x, row_bit):
    upper = lax.broadcasted_iota(jnp.int32, (8, 128), 0) >= 4
    tiles = [x[8 * i : 8 * i + 8] for i in range(16)]
    bit = 1 << (row_bit - 3)
    out = [None] * 16
    for i in range(16):
        if not i & bit:
            a, b = tiles[i], tiles[i | bit]
            out[i] = jnp.where(upper, pltpu.roll(b, 4, 0), a)
            out[i | bit] = jnp.where(upper, b, pltpu.roll(a, 4, 0))
    return jnp.concatenate(out, 0)


def hops(k):
    in_y = 1 if k & 1 else (2 if k & 16 else 0)
    in_x = 1 if k & 4 else (2 if k & 8 else 0)
    return 2 * (in_x + in_y) + ((k >> 1) & 1)


IN_PLANE = sorted(range(1, 32), key=hops, reverse=True)
IN_LINE = [k >> 1 for k in IN_PLANE if k < 16 and not k & 1]


def kernel(
    scale, ket_ref, bra_ref, gate_hbm, outs,
    states, gates, send_a, recv_a, send_b, recv_b, chunks, partial, packed, column,
    line_out, line_in, rows_out, rows_in, extra, share, final,
    in_sem, a_send, a_recv, b_send, b_recv, c_send, c_recv, z_send, z_recv, l_send, l_recv, q_send, q_recv, f_send, f_recv, line, near, mid, far,
):
    hi, lo = lax.axis_index("hi"), lax.axis_index("lo")
    z, y = lo & 31, lo >> 5
    me = hi * 2 + y
    held = ((hi & 7) >> 1) + ((1 - (hi & 1)) << 2)
    loads = [
        pltpu.make_async_copy(gate_hbm, gates, in_sem.at[2]),
        pltpu.make_async_copy(ket_ref, states.at[0], in_sem.at[0]),
        pltpu.make_async_copy(bra_ref, states.at[1], in_sem.at[1]),
    ]
    for load in loads:
        load.start()

    def ring(step):
        return (hi, (lo & 32) + ((z + step) & 31))

    def in_plane(k):
        return (hi ^ (k >> 1), lo ^ ((k & 1) * 32))

    barrier = pltpu.get_barrier_semaphore()

    def greet(device):
        pl.semaphore_signal(barrier, inc=1, device_id=device, device_id_type=MESH)

    greet((hi ^ 4, lo ^ 2))
    for step in (2, -2, 1, -1):
        greet(ring(step))
    for k in IN_LINE:
        greet((hi ^ k, lo))
    for k in (16, 17, 1):
        greet(in_plane(k))
    extra[...] = jnp.zeros((2, 8, 128), F32)
    loads[0].wait()

    def layer_setup(layer, bits, on_rows):
        picked, mask = picks(layer, bits), rest_mask(layer, bits)
        return picked, mask, spread_gate(gates[layer], layer, bits, picked, mask, on_rows)

    pick4, mask4, gate4 = layer_setup(4, ROWS, True)
    pick3, mask3, gate3 = layer_setup(3, LANES, False)

    loads[1].wait()
    loads[2].wait()
    x5 = [swap_sublane(states[s, pl.ds(c, 128, stride=2), :], 6) for s in range(2) for c in range(2)]
    x4 = undo_on_rows(gate4, x5)
    x3 = undo_on_lanes(gate3, x4)
    mine = ((hi >> 2) & 1) * 2 + ((lo >> 1) & 1)
    for i in range(4):
        ready = swap_lane(x3[i], 5, 3)
        for block in range(4):
            send_a[block, i] = ready[32 * block : 32 * block + 32]

    pl.semaphore_wait(barrier, 15)

    def copy_a(d):
        return pltpu.make_async_remote_copy(
            send_a.at[mine ^ d], recv_a.at[mine], a_send.at[d], a_recv.at[d],
            device_id=(hi ^ (4 if d & 2 else 0), lo ^ (2 if d & 1 else 0)), device_id_type=MESH,
        )

    copy_a(3).start()
    copy_a(1).start()
    copy_a(2).start()
    for k in IN_LINE:
        pl.semaphore_signal(line, inc=1, device_id=(hi ^ k, lo), device_id_type=MESH)
    for step in (2, -2):
        pl.semaphore_signal(near, inc=1, device_id=ring(step), device_id_type=MESH)
    recv_a[mine] = send_a[mine]

    def all_of(ref, sem):
        pltpu.make_async_copy(ref, ref, sem).wait()

    first = to_chunks(outer_on_rows(x5[2:], x4[:2]), 4, ROWS, pick4, mask4, 0, True)
    first += to_chunks(outer_on_lanes(x4[2:], x3[:2]), 3, LANES, pick3, mask3, 3, True)
    chunks[...] = first.reshape(32, 8, 128)
    partial[me] = chunks[me]
    pl.semaphore_wait(line, 7)
    pl.semaphore_wait(near, 2)
    for step in (4, -4):
        pl.semaphore_signal(mid, inc=1, device_id=ring(step), device_id_type=MESH)
    for k in IN_PLANE:
        pltpu.make_async_remote_copy(
            chunks.at[me ^ k], partial.at[me], c_send, c_recv, device_id=in_plane(k), device_id_type=MESH,
        ).start()

    pick2, mask2, gate2 = layer_setup(2, ROWS_MIXED, True)
    pick1, mask1, gate1 = layer_setup(1, LANES, False)
    pick0, mask0, gate0 = layer_setup(0, ROWS, True)
    pl.semaphore_wait(mid, 2)
    for step in (8, -8):
        pl.semaphore_signal(far, inc=1, device_id=ring(step), device_id_type=MESH)

    for d in (1, 2, 3):
        copy_a(d).wait()
    x = [jnp.concatenate([recv_a[block, i] for block in range(4)], 0) for i in range(4)]
    x = [swap_lane(v, 5, 3) for v in x]
    mixed = [swap_lane(swap_lane(swap_lane(v, 3, 4), 4, 5), 5, 6) for v in x]

    def send_line(layer, value):
        line_out[layer] = value.reshape(8, 8, 128)
        for k in IN_LINE:
            pltpu.make_async_remote_copy(
                line_out.at[layer, (hi & 7) ^ k], line_in.at[layer, hi & 7], l_send.at[layer], l_recv.at[layer],
                device_id=(hi ^ k, lo), device_id_type=MESH,
            ).start()
        line_in[layer, hi & 7] = line_out[layer, hi & 7]

    x2 = undo_on_rows(gate2, mixed)
    turned = [swap_lane(swap_lane(swap_lane(v, 3, 4), 4, 5), 5, 6) for v in x2]
    x1 = undo_on_lanes(gate1, turned)
    send_line(2, to_chunks(outer_on_rows(mixed[2:], x2[:2]), 2, ROWS_MIXED, pick2, mask2, 0, False))
    x0 = undo_on_rows(gate0, x1)
    send_line(1, to_chunks(outer_on_lanes(turned[2:], x1[:2]), 1, LANES, pick1, mask1, 0, False))
    send_line(0, to_chunks(outer_on_rows(x1[2:], x0[:2]), 0, ROWS, pick0, mask0, 0, False))

    own = ((hi >> 1) & 1) * 4 + (lo & 1) * 2 + (hi & 1)
    for i in range(4):
        ready = swap_sublane(swap_lane(swap_lane(x0[i], 5, 6), 4, 0), 3)
        for block in range(8):
            for top in range(2):
                send_b[block, i, top] = ready[64 * top + 8 * block : 64 * top + 8 * block + 8]
    recv_b[own] = send_b[own]
    copies_b = []
    for d in range(1, 8):
        copy = pltpu.make_async_remote_copy(
            send_b.at[own ^ d], recv_b.at[own], b_send.at[d], b_recv.at[d],
            device_id=(hi ^ ((2 if d & 4 else 0) + (d & 1)), lo ^ (1 if d & 2 else 0)), device_id_type=MESH,
        )
        copy.start()
        copies_b.append(copy)

    sub = lax.broadcasted_iota(jnp.int32, (8, 128), 0)
    all_of(partial.at[pl.ds(0, 31)], c_recv)
    sum1 = jnp.sum(partial[...], 0)
    turned1 = pltpu.roll(sum1, 4, 0)
    for q in range(2):
        three, four = (turned1, sum1) if q else (sum1, turned1)
        packed[q] = jnp.where(sub == 3, three, jnp.where(sub == 4, four, 0.0))
    pl.semaphore_wait(far, 2)

    def column_copy(q):
        return pltpu.make_async_remote_copy(
            packed.at[q], column.at[z], z_send.at[q], z_recv,
            device_id=(hi, (lo & 32) + held + (hi & 8) + 16 * q), device_id_type=MESH,
        )

    sums = []
    for layer in (2, 1, 0):
        all_of(line_in.at[layer, pl.ds(0, 7)], l_recv.at[layer])
        sums.insert(0, jnp.sum(line_in[layer], 0))
    for q in range(4):
        value = jnp.zeros((8, 128), F32)
        for layer in range(3):
            shift = (layer - q) % 8
            value = jnp.where(sub & 3 == layer, pltpu.roll(sums[layer], shift, 0) if shift else sums[layer], value)
        rows_out[q] = value

    def row_copy(q):
        return pltpu.make_async_remote_copy(
            rows_out.at[q], rows_in.at[z], q_send.at[q], q_recv,
            device_id=(hi, (lo & 32) + held + 8 * q), device_id_type=MESH,
        )

    for q in range(4):
        @pl.when(z != held + 8 * q)
        def _():
            row_copy(q).start()

        @pl.when(z == held + 8 * q)
        def _():
            rows_in[z] = rows_out[q]

    for q in range(2):
        @pl.when(z != held + (hi & 8) + 16 * q)
        def _():
            column_copy(q).start()

        @pl.when(z == held + (hi & 8) + 16 * q)
        def _():
            column[z] = packed[q]

    for copy in copies_b:
        copy.wait()
    for i in range(4):
        v = jnp.concatenate([recv_b[block, i, top] for top in range(2) for block in range(8)], 0)
        v = swap_lane(swap_lane(swap_sublane(v, 3), 4, 0), 5, 6)
        outs[pl.ds(256 * (i // 2) + i % 2, 128, stride=2), :] = swap_sublane(v, 6)
    all_of(chunks.at[pl.ds(0, 31)], c_send)
    for layer in range(3):
        all_of(line_out.at[layer, pl.ds(0, 7)], l_send.at[layer])
    for q in range(2):
        @pl.when(z != held + (hi & 8) + 16 * q)
        def _():
            column_copy(q).wait_send()

    for q in range(4):
        @pl.when(z != held + 8 * q)
        def _():
            row_copy(q).wait_send()

    sink = (z & 7) == held
    slot = (hi >> 3) * 2 + y

    @pl.when((z & 15) == held + (hi & 8))
    def _():
        all_of(column.at[pl.ds(0, 31)], z_recv)
        extra[y] = jnp.sum(column[...], 0)

    @pl.when(sink)
    def _():
        all_of(rows_in.at[pl.ds(0, 31)], q_recv)
        total = jnp.sum(rows_in[...], 0)
        share[0] = jnp.where(sub < 3, total, 0.0) + extra[0]
        share[1] = jnp.where(sub < 3, pltpu.roll(total, 4, 0), 0.0) + extra[1]
        for k in IN_PLANE:
            pltpu.make_async_remote_copy(
                share.at[y ^ (k & 1)], final.at[slot], f_send, f_recv, device_id=in_plane(k), device_id_type=MESH,
            ).start()
        final[slot] = share[y]
        all_of(final.at[pl.ds(0, 3)], f_recv)

    @pl.when(jnp.logical_not(sink))
    def _():
        all_of(final.at[pl.ds(0, 4)], f_recv)

    outs[512:520, :] = jnp.sum(final[...], 0) * scale
    @pl.when(sink)
    def _():
        all_of(column.at[pl.ds(0, 31)], f_send)


def put_kernel(whole, ket, bra, grad, slim, sem):
    copies = [
        pltpu.make_async_copy(whole.at[pl.ds(0, 256)], ket, sem.at[0]),
        pltpu.make_async_copy(whole.at[pl.ds(256, 256)], bra, sem.at[1]),
        pltpu.make_async_copy(slim, grad, sem.at[2]),
    ]
    for layer in range(5):
        slim[layer] = whole[512 + layer : 513 + layer, :]
    for copy in copies:
        copy.start()
    for copy in copies:
        copy.wait()


def body(ket_state, bra_state, gate_matrices):
    scale = (64 / (16384 * lax.axis_size("hi") * lax.axis_size("lo"))) ** 0.5
    amplitudes = ket_state.shape[1]
    hbm = pl.BlockSpec(memory_space=pltpu.HBM)
    dma = pltpu.SemaphoreType.DMA
    regular = pltpu.SemaphoreType.REGULAR
    whole = pl.pallas_call(
        functools.partial(kernel, scale),
        out_shape=jax.ShapeDtypeStruct((520, 128), F32),
        in_specs=[hbm] * 3,
        out_specs=pl.BlockSpec(memory_space=pltpu.VMEM),
        scratch_shapes=[
            pltpu.VMEM((2, 256, 128), F32),
            pltpu.VMEM((5, 64, 128), F32),
            pltpu.VMEM((4, 4, 32, 128), F32),
            pltpu.VMEM((4, 4, 32, 128), F32),
            pltpu.VMEM((8, 4, 2, 8, 128), F32),
            pltpu.VMEM((8, 4, 2, 8, 128), F32),
            pltpu.VMEM((32, 8, 128), F32),
            pltpu.VMEM((32, 8, 128), F32),
            pltpu.VMEM((2, 8, 128), F32),
            pltpu.VMEM((32, 8, 128), F32),
            pltpu.VMEM((3, 8, 8, 128), F32),
            pltpu.VMEM((3, 8, 8, 128), F32),
            pltpu.VMEM((4, 8, 128), F32),
            pltpu.VMEM((32, 8, 128), F32),
            pltpu.VMEM((2, 8, 128), F32),
            pltpu.VMEM((2, 8, 128), F32),
            pltpu.VMEM((4, 8, 128), F32),
            dma((3,)), dma((4,)), dma((4,)), dma((8,)), dma((8,)),
            dma, dma, dma((2,)), dma, dma((3,)), dma((3,)), dma((4,)), dma, dma, dma,
            regular, regular, regular, regular,
        ],
        compiler_params=pltpu.CompilerParams(collective_id=0, has_side_effects=True, vmem_limit_bytes=40 * 2**20),
        name="window",
    )(
        *(
            pltpu.with_memory_space_constraint(v, pltpu.HBM)
            for v in (
                ket_state.reshape(2, 128, 128).transpose(1, 0, 2).reshape(256, 128),
                bra_state.reshape(2, 128, 128).transpose(1, 0, 2).reshape(256, 128),
                gate_matrices,
            )
        ),
    )
    state = jax.ShapeDtypeStruct((256, 128), F32)
    slim = jax.ShapeDtypeStruct((5, 1, 128), F32)
    ket, bra, grad = pl.pallas_call(
        put_kernel,
        out_shape=(state, state, slim),
        in_specs=[pl.BlockSpec(memory_space=pltpu.VMEM)],
        out_specs=(hbm,) * 3,
        scratch_shapes=[pltpu.VMEM((5, 1, 128), F32), dma((3,))],
        name="put",
    )(pltpu.with_memory_space_constraint(whole, pltpu.VMEM))
    ket, bra = (v.reshape(128, 2, 128).transpose(1, 0, 2).reshape(2, amplitudes) for v in (ket, bra))
    return ket, bra, grad


def solution(mesh):
    placed = (P(None, ("hi", "lo")), P(None, ("hi", "lo")), P())
    return jax.shard_map(
        body,
        mesh=mesh,
        in_specs=placed,
        out_specs=(P(None, ("hi", "lo")), P(None, ("hi", "lo")), P(None, "lo", None)),
        check_vma=False,
    )
```

```python
import functools

import jax
import jax.numpy as jnp
from jax import lax
from jax.experimental import pallas as pl
from jax.experimental.pallas import tpu as pltpu
from jax.sharding import PartitionSpec as P

F32 = jnp.float32
BF16 = jnp.bfloat16
MESH = pl.DeviceIdType.MESH
LOCAL_BITS = 14
FIRST = (8, 0, 4, 1, 7)
ORDER = (2, 0, 5, 1, 4, 3)
ROWS = (7, 8, 13, 10, 11, 12, 9)
LANES = (0, 1, 2, 3, 4, 5, 6)
ROWS_MIXED = (7, 8, 13, 4, 5, 6, 9)
NN = (((1,), (0,)), ((), ()))
NT = (((1,), (1,)), ((), ()))
TN = (((0,), (0,)), ((), ()))


def target_bits(layer):
    return [(FIRST[layer] + ORDER[(j + layer) % 6]) % LOCAL_BITS for j in range(6)]


def mm(a, b, dims):
    return lax.dot_general(a, b, dims, preferred_element_type=F32)


def halves(x):
    top = x.astype(BF16)
    return top, (x - top.astype(F32)).astype(BF16)


def mm3(a, b, dims):
    return mm(a[0], b[0], dims) + mm(a[0], b[1], dims) + mm(a[1], b[0], dims)


def gate_code(index, layer, bits):
    code = None
    for j, target in enumerate(target_bits(layer)):
        term = ((index >> bits.index(target)) & 1) << j
        code = term if code is None else code + term
    return code


def rest_position(layer, bits):
    targets = target_bits(layer)
    return [i for i, bit in enumerate(bits) if bit not in targets][0]


def holder(z):
    return ((z & 3) << 1) + 1 - (z >> 2)


def picks(layer, bits):
    row = lax.broadcasted_iota(jnp.int32, (256, 128), 0)
    column = lax.broadcasted_iota(jnp.int32, (256, 128), 1)
    code = gate_code(row & 127, layer, bits) + ((row >> 7) << 6)
    return (code == column).astype(F32).astype(BF16)


def rest_mask(layer, bits):
    i = lax.broadcasted_iota(jnp.int32, (128, 128), 0)
    j = lax.broadcasted_iota(jnp.int32, (128, 128), 1)
    return (((i ^ j) >> rest_position(layer, bits)) & 1) == 0


def spread_gate(u, layer, bits, picked, mask, on_rows):
    row = lax.broadcasted_iota(jnp.int32, (128, 64), 0)
    column = lax.broadcasted_iota(jnp.int32, (128, 64), 1)
    chooser = (gate_code(row, layer, bits) == column).astype(F32).astype(BF16)
    u_parts = halves(u)
    tall = jnp.concatenate([mm(chooser, part, NN).astype(BF16) for part in u_parts], 0)
    out = []
    if on_rows:
        wide = mm(picked, tall, NT)
        for part in range(2):
            columns = slice(128 * part, 128 * part + 128)
            real = jnp.where(mask, wide[:128, columns], 0.0)
            imag = jnp.where(mask, wide[128:, columns], 0.0)
            out.append(jnp.concatenate([jnp.concatenate([real, imag], 1), jnp.concatenate([-imag, real], 1)], 0).astype(BF16))
    else:
        wide = mm(tall, picked, NT)
        for part in range(2):
            rows = slice(128 * part, 128 * part + 128)
            real = jnp.where(mask, wide[rows, :128], 0.0)
            imag = jnp.where(mask, wide[rows, 128:], 0.0)
            out.append(jnp.concatenate([jnp.concatenate([real, -imag], 1), jnp.concatenate([imag, real], 1)], 0).astype(BF16))
    return tuple(out)


def undo_on_rows(gate, x):
    flat = jnp.concatenate([jnp.concatenate([x[0], x[2]], 1), jnp.concatenate([x[1], x[3]], 1)], 0)
    y = mm3(gate, halves(flat), NN)
    return [y[:128, :128], y[128:, :128], y[:128, 128:], y[128:, 128:]]


def undo_on_lanes(gate, x):
    flat = jnp.concatenate([jnp.concatenate([x[0], x[1]], 1), jnp.concatenate([x[2], x[3]], 1)], 0)
    y = mm3(halves(flat), gate, NN)
    return [y[:128, :128], y[:128, 128:], y[128:, :128], y[128:, 128:]]


def outer_on_rows(bra, ket):
    left = jnp.concatenate(bra, 1)
    right = jnp.concatenate([jnp.concatenate([ket[0], ket[1]], 1), jnp.concatenate([ket[1], -ket[0]], 1)], 0)
    return mm3(halves(left), halves(right), NT)


def outer_on_lanes(bra, ket):
    left = jnp.concatenate(bra, 0)
    right = jnp.concatenate([jnp.concatenate([ket[0], ket[1]], 1), jnp.concatenate([ket[1], -ket[0]], 1)], 0)
    return mm3(halves(left), halves(right), TN)


def to_chunks(wide, layer, bits, picked, mask, slot, by_plane):
    kept = jnp.concatenate([jnp.where(mask, wide[:, :128], 0.0), jnp.where(mask, wide[:, 128:], 0.0)], 1)
    both = mm(jnp.concatenate(halves(kept), 0), picked, NN)
    narrow = jnp.concatenate(halves(both[:128] + both[128:]), 0)
    shape = (256 if by_plane else 64, 256)
    row = lax.broadcasted_iota(jnp.int32, shape, 0)
    column = lax.broadcasted_iota(jnp.int32, shape, 1)
    code = gate_code(column & 127, layer, bits)
    if by_plane:
        place = (((code & 8) + holder(code & 7)) << 4) + ((code >> 5) << 3) + (((code >> 4) & 1) << 2) + slot
    else:
        place = (holder(code & 7) << 3) + (code >> 3)
    return mm((row == place).astype(F32).astype(BF16), narrow, NN)


def swap_lane(x, row_bit, lane_bit):
    size, step = 1 << row_bit, 1 << lane_bit
    lane = lax.broadcasted_iota(jnp.int32, (size, 128), 1)
    upper = ((lane >> lane_bit) & 1) == 1
    out = []
    for base in range(0, 128, 2 * size):
        a, b = x[base : base + size], x[base + size : base + 2 * size]
        out.append(jnp.where(upper, pltpu.roll(b, step, 1), a))
        out.append(jnp.where(upper, b, pltpu.roll(a, 128 - step, 1)))
    return jnp.concatenate(out, 0)


def swap_sublane(x, row_bit):
    upper = lax.broadcasted_iota(jnp.int32, (8, 128), 0) >= 4
    tiles = [x[8 * i : 8 * i + 8] for i in range(16)]
    bit = 1 << (row_bit - 3)
    out = [None] * 16
    for i in range(16):
        if not i & bit:
            a, b = tiles[i], tiles[i | bit]
            out[i] = jnp.where(upper, pltpu.roll(b, 4, 0), a)
            out[i | bit] = jnp.where(upper, b, pltpu.roll(a, 4, 0))
    return jnp.concatenate(out, 0)


def hops(k):
    in_y = 1 if k & 1 else (2 if k & 16 else 0)
    in_x = 1 if k & 4 else (2 if k & 8 else 0)
    return 2 * (in_x + in_y) + ((k >> 1) & 1)


IN_PLANE = sorted(range(1, 32), key=hops, reverse=True)
IN_LINE = [k >> 1 for k in IN_PLANE if k < 16 and not k & 1]


def kernel(
    scale, ket_ref, bra_ref, gate_hbm, outs,
    states, gates, send_a, recv_a, send_b, recv_b, chunks, partial, packed, column,
    line_out, line_in, rows_out, rows_in, extra, share, final,
    in_sem, a_send, a_recv, b_send, b_recv, c_send, c_recv, z_send, z_recv, l_send, l_recv, q_send, q_recv, f_send, f_recv, line, near, mid, far,
):
    hi, lo = lax.axis_index("hi"), lax.axis_index("lo")
    z, y = lo & 31, lo >> 5
    me = hi * 2 + y
    held = ((hi & 7) >> 1) + ((1 - (hi & 1)) << 2)
    loads = [
        pltpu.make_async_copy(gate_hbm, gates, in_sem.at[2]),
        pltpu.make_async_copy(ket_ref, states.at[0], in_sem.at[0]),
        pltpu.make_async_copy(bra_ref, states.at[1], in_sem.at[1]),
    ]
    for load in loads:
        load.start()

    def ring(step):
        return (hi, (lo & 32) + ((z + step) & 31))

    def in_plane(k):
        return (hi ^ (k >> 1), lo ^ ((k & 1) * 32))

    barrier = pltpu.get_barrier_semaphore()

    def greet(device):
        pl.semaphore_signal(barrier, inc=1, device_id=device, device_id_type=MESH)

    greet((hi ^ 4, lo ^ 2))
    for step in (2, -2, 1, -1):
        greet(ring(step))
    for k in IN_LINE:
        greet((hi ^ k, lo))
    for k in (16, 17, 1):
        greet(in_plane(k))
    extra[...] = jnp.zeros((2, 8, 128), F32)
    loads[0].wait()

    def layer_setup(layer, bits, on_rows):
        picked, mask = picks(layer, bits), rest_mask(layer, bits)
        return picked, mask, spread_gate(gates[layer], layer, bits, picked, mask, on_rows)

    pick4, mask4, gate4 = layer_setup(4, ROWS, True)
    pick3, mask3, gate3 = layer_setup(3, LANES, False)

    loads[1].wait()
    loads[2].wait()
    x5 = [swap_sublane(states[s, pl.ds(c, 128, stride=2), :], 6) for s in range(2) for c in range(2)]
    x4 = undo_on_rows(gate4, x5)
    x3 = undo_on_lanes(gate3, x4)
    mine = ((hi >> 2) & 1) * 2 + ((lo >> 1) & 1)
    for i in range(4):
        ready = swap_lane(x3[i], 5, 3)
        for block in range(4):
            send_a[block, i] = ready[32 * block : 32 * block + 32]

    pl.semaphore_wait(barrier, 15)

    def copy_a(d, s):
        both = pl.ds(2 * s, 2)
        return pltpu.make_async_remote_copy(
            send_a.at[mine ^ d, both], recv_a.at[mine, both], a_send.at[s, d], a_recv.at[s, d],
            device_id=(hi ^ (4 if d & 2 else 0), lo ^ (2 if d & 1 else 0)), device_id_type=MESH,
        )

    for s in range(2):
        for d in (3, 1, 2):
            copy_a(d, s).start()
    for k in IN_LINE:
        pl.semaphore_signal(line, inc=1, device_id=(hi ^ k, lo), device_id_type=MESH)
    for step in (2, -2):
        pl.semaphore_signal(near, inc=1, device_id=ring(step), device_id_type=MESH)
    recv_a[mine] = send_a[mine]

    def all_of(ref, sem):
        pltpu.make_async_copy(ref, ref, sem).wait()

    first = to_chunks(outer_on_rows(x5[2:], x4[:2]), 4, ROWS, pick4, mask4, 0, True)
    first += to_chunks(outer_on_lanes(x4[2:], x3[:2]), 3, LANES, pick3, mask3, 3, True)
    chunks[...] = first.reshape(32, 8, 128)
    partial[me] = chunks[me]
    pl.semaphore_wait(line, 7)
    pl.semaphore_wait(near, 2)
    for step in (4, -4):
        pl.semaphore_signal(mid, inc=1, device_id=ring(step), device_id_type=MESH)
    for k in IN_PLANE:
        pltpu.make_async_remote_copy(
            chunks.at[me ^ k], partial.at[me], c_send, c_recv, device_id=in_plane(k), device_id_type=MESH,
        ).start()

    pick2, mask2, gate2 = layer_setup(2, ROWS_MIXED, True)
    pick1, mask1, gate1 = layer_setup(1, LANES, False)
    pick0, mask0, gate0 = layer_setup(0, ROWS, True)
    pl.semaphore_wait(mid, 2)
    for step in (8, -8):
        pl.semaphore_signal(far, inc=1, device_id=ring(step), device_id_type=MESH)

    def arrived(s):
        for d in (3, 1, 2):
            copy_a(d, s).wait()
        x = [jnp.concatenate([recv_a[block, 2 * s + c] for block in range(4)], 0) for c in range(2)]
        return turn([swap_lane(v, 5, 3) for v in x])

    def turn(x):
        return [swap_lane(swap_lane(swap_lane(v, 3, 4), 4, 5), 5, 6) for v in x]

    def one_on_rows(gate, x):
        out = mm3(gate, halves(jnp.concatenate(x, 0)), NN)
        return [out[:128], out[128:]]

    def one_on_lanes(gate, x):
        out = mm3(halves(jnp.concatenate(x, 1)), gate, NN)
        return [out[:, :128], out[:, 128:]]

    def send_line(layer, value):
        line_out[layer] = value.reshape(8, 8, 128)
        for k in IN_LINE:
            pltpu.make_async_remote_copy(
                line_out.at[layer, (hi & 7) ^ k], line_in.at[layer, hi & 7], l_send.at[layer], l_recv.at[layer],
                device_id=(hi ^ k, lo), device_id_type=MESH,
            ).start()
        line_in[layer, hi & 7] = line_out[layer, hi & 7]

    ket2 = one_on_rows(gate2, arrived(0))
    ket1 = one_on_lanes(gate1, turn(ket2))
    ket0 = one_on_rows(gate0, ket1)
    bra3 = arrived(1)
    send_line(2, to_chunks(outer_on_rows(bra3, ket2), 2, ROWS_MIXED, pick2, mask2, 0, False))
    bra2 = turn(one_on_rows(gate2, bra3))
    send_line(1, to_chunks(outer_on_lanes(bra2, ket1), 1, LANES, pick1, mask1, 0, False))
    bra1 = one_on_lanes(gate1, bra2)
    send_line(0, to_chunks(outer_on_rows(bra1, ket0), 0, ROWS, pick0, mask0, 0, False))
    x0 = ket0 + one_on_rows(gate0, bra1)

    own = ((hi >> 1) & 1) * 4 + (lo & 1) * 2 + (hi & 1)
    for i in range(4):
        ready = swap_sublane(swap_lane(swap_lane(x0[i], 5, 6), 4, 0), 3)
        for block in range(8):
            for top in range(2):
                send_b[block, i, top] = ready[64 * top + 8 * block : 64 * top + 8 * block + 8]
    recv_b[own] = send_b[own]
    copies_b = []
    for d in range(1, 8):
        copy = pltpu.make_async_remote_copy(
            send_b.at[own ^ d], recv_b.at[own], b_send.at[d], b_recv.at[d],
            device_id=(hi ^ ((2 if d & 4 else 0) + (d & 1)), lo ^ (1 if d & 2 else 0)), device_id_type=MESH,
        )
        copy.start()
        copies_b.append(copy)

    sub = lax.broadcasted_iota(jnp.int32, (8, 128), 0)
    all_of(partial.at[pl.ds(0, 31)], c_recv)
    sum1 = jnp.sum(partial[...], 0)
    turned1 = pltpu.roll(sum1, 4, 0)
    for q in range(2):
        three, four = (turned1, sum1) if q else (sum1, turned1)
        packed[q] = jnp.where(sub == 3, three, jnp.where(sub == 4, four, 0.0))
    pl.semaphore_wait(far, 2)

    def column_copy(q):
        return pltpu.make_async_remote_copy(
            packed.at[q], column.at[z], z_send.at[q], z_recv,
            device_id=(hi, (lo & 32) + held + (hi & 8) + 16 * q), device_id_type=MESH,
        )

    sums = []
    for layer in (2, 1, 0):
        all_of(line_in.at[layer, pl.ds(0, 7)], l_recv.at[layer])
        sums.insert(0, jnp.sum(line_in[layer], 0))
    for q in range(4):
        value = jnp.zeros((8, 128), F32)
        for layer in range(3):
            shift = (layer - q) % 8
            value = jnp.where(sub & 3 == layer, pltpu.roll(sums[layer], shift, 0) if shift else sums[layer], value)
        rows_out[q] = value

    def row_copy(q):
        return pltpu.make_async_remote_copy(
            rows_out.at[q], rows_in.at[z], q_send.at[q], q_recv,
            device_id=(hi, (lo & 32) + held + 8 * q), device_id_type=MESH,
        )

    for q in range(4):
        @pl.when(z != held + 8 * q)
        def _():
            row_copy(q).start()

        @pl.when(z == held + 8 * q)
        def _():
            rows_in[z] = rows_out[q]

    for q in range(2):
        @pl.when(z != held + (hi & 8) + 16 * q)
        def _():
            column_copy(q).start()

        @pl.when(z == held + (hi & 8) + 16 * q)
        def _():
            column[z] = packed[q]

    for copy in copies_b:
        copy.wait()
    for i in range(4):
        v = jnp.concatenate([recv_b[block, i, top] for top in range(2) for block in range(8)], 0)
        v = swap_lane(swap_lane(swap_sublane(v, 3), 4, 0), 5, 6)
        outs[pl.ds(256 * (i // 2) + i % 2, 128, stride=2), :] = swap_sublane(v, 6)
    all_of(chunks.at[pl.ds(0, 31)], c_send)
    for layer in range(3):
        all_of(line_out.at[layer, pl.ds(0, 7)], l_send.at[layer])
    for q in range(2):
        @pl.when(z != held + (hi & 8) + 16 * q)
        def _():
            column_copy(q).wait_send()

    for q in range(4):
        @pl.when(z != held + 8 * q)
        def _():
            row_copy(q).wait_send()

    sink = (z & 7) == held
    slot = (hi >> 3) * 2 + y

    @pl.when((z & 15) == held + (hi & 8))
    def _():
        all_of(column.at[pl.ds(0, 31)], z_recv)
        extra[y] = jnp.sum(column[...], 0)

    @pl.when(sink)
    def _():
        all_of(rows_in.at[pl.ds(0, 31)], q_recv)
        total = jnp.sum(rows_in[...], 0)
        share[0] = jnp.where(sub < 3, total, 0.0) + extra[0]
        share[1] = jnp.where(sub < 3, pltpu.roll(total, 4, 0), 0.0) + extra[1]
        for k in IN_PLANE:
            pltpu.make_async_remote_copy(
                share.at[y ^ (k & 1)], final.at[slot], f_send, f_recv, device_id=in_plane(k), device_id_type=MESH,
            ).start()
        final[slot] = share[y]
        all_of(final.at[pl.ds(0, 3)], f_recv)

    @pl.when(jnp.logical_not(sink))
    def _():
        all_of(final.at[pl.ds(0, 4)], f_recv)

    outs[512:520, :] = jnp.sum(final[...], 0) * scale
    @pl.when(sink)
    def _():
        all_of(column.at[pl.ds(0, 31)], f_send)


def put_kernel(whole, ket, bra, grad, slim, sem):
    copies = [
        pltpu.make_async_copy(whole.at[pl.ds(0, 256)], ket, sem.at[0]),
        pltpu.make_async_copy(whole.at[pl.ds(256, 256)], bra, sem.at[1]),
        pltpu.make_async_copy(slim, grad, sem.at[2]),
    ]
    for layer in range(5):
        slim[layer] = whole[512 + layer : 513 + layer, :]
    for copy in copies:
        copy.start()
    for copy in copies:
        copy.wait()


def body(ket_state, bra_state, gate_matrices):
    scale = (64 / (16384 * lax.axis_size("hi") * lax.axis_size("lo"))) ** 0.5
    amplitudes = ket_state.shape[1]
    hbm = pl.BlockSpec(memory_space=pltpu.HBM)
    dma = pltpu.SemaphoreType.DMA
    regular = pltpu.SemaphoreType.REGULAR
    whole = pl.pallas_call(
        functools.partial(kernel, scale),
        out_shape=jax.ShapeDtypeStruct((520, 128), F32),
        in_specs=[hbm] * 3,
        out_specs=pl.BlockSpec(memory_space=pltpu.VMEM),
        scratch_shapes=[
            pltpu.VMEM((2, 256, 128), F32),
            pltpu.VMEM((5, 64, 128), F32),
            pltpu.VMEM((4, 4, 32, 128), F32),
            pltpu.VMEM((4, 4, 32, 128), F32),
            pltpu.VMEM((8, 4, 2, 8, 128), F32),
            pltpu.VMEM((8, 4, 2, 8, 128), F32),
            pltpu.VMEM((32, 8, 128), F32),
            pltpu.VMEM((32, 8, 128), F32),
            pltpu.VMEM((2, 8, 128), F32),
            pltpu.VMEM((32, 8, 128), F32),
            pltpu.VMEM((3, 8, 8, 128), F32),
            pltpu.VMEM((3, 8, 8, 128), F32),
            pltpu.VMEM((4, 8, 128), F32),
            pltpu.VMEM((32, 8, 128), F32),
            pltpu.VMEM((2, 8, 128), F32),
            pltpu.VMEM((2, 8, 128), F32),
            pltpu.VMEM((4, 8, 128), F32),
            dma((3,)), dma((2, 4)), dma((2, 4)), dma((8,)), dma((8,)),
            dma, dma, dma((2,)), dma, dma((3,)), dma((3,)), dma((4,)), dma, dma, dma,
            regular, regular, regular, regular,
        ],
        compiler_params=pltpu.CompilerParams(collective_id=0, has_side_effects=True, vmem_limit_bytes=40 * 2**20),
        name="window",
    )(
        *(
            pltpu.with_memory_space_constraint(v, pltpu.HBM)
            for v in (
                ket_state.reshape(2, 128, 128).transpose(1, 0, 2).reshape(256, 128),
                bra_state.reshape(2, 128, 128).transpose(1, 0, 2).reshape(256, 128),
                gate_matrices,
            )
        ),
    )
    state = jax.ShapeDtypeStruct((256, 128), F32)
    slim = jax.ShapeDtypeStruct((5, 1, 128), F32)
    ket, bra, grad = pl.pallas_call(
        put_kernel,
        out_shape=(state, state, slim),
        in_specs=[pl.BlockSpec(memory_space=pltpu.VMEM)],
        out_specs=(hbm,) * 3,
        scratch_shapes=[pltpu.VMEM((5, 1, 128), F32), dma((3,))],
        name="put",
    )(pltpu.with_memory_space_constraint(whole, pltpu.VMEM))
    ket, bra = (v.reshape(128, 2, 128).transpose(1, 0, 2).reshape(2, amplitudes) for v in (ket, bra))
    return ket, bra, grad


def solution(mesh):
    placed = (P(None, ("hi", "lo")), P(None, ("hi", "lo")), P())
    return jax.shard_map(
        body,
        mesh=mesh,
        in_specs=placed,
        out_specs=(P(None, ("hi", "lo")), P(None, ("hi", "lo")), P(None, "lo", None)),
        check_vma=False,
    )
```

```python
import functools

import jax
import jax.numpy as jnp
from jax import lax
from jax.experimental import pallas as pl
from jax.experimental.pallas import tpu as pltpu
from jax.sharding import PartitionSpec as P

F32 = jnp.float32
BF16 = jnp.bfloat16
MESH = pl.DeviceIdType.MESH
LOCAL_BITS = 14
FIRST = (8, 0, 4, 1, 7)
ORDER = (2, 0, 5, 1, 4, 3)
ROWS = (7, 8, 13, 10, 11, 12, 9)
LANES = (0, 1, 2, 3, 4, 5, 6)
ROWS_MIXED = (7, 8, 13, 4, 5, 6, 9)
NN = (((1,), (0,)), ((), ()))
NT = (((1,), (1,)), ((), ()))
TN = (((0,), (0,)), ((), ()))


def target_bits(layer):
    return [(FIRST[layer] + ORDER[(j + layer) % 6]) % LOCAL_BITS for j in range(6)]


def mm(a, b, dims):
    return lax.dot_general(a, b, dims, preferred_element_type=F32)


def halves(x):
    top = x.astype(BF16)
    return top, (x - top.astype(F32)).astype(BF16)


def mm3(a, b, dims):
    return mm(a[0], b[0], dims) + mm(a[0], b[1], dims) + mm(a[1], b[0], dims)


def gate_code(index, layer, bits):
    code = None
    for j, target in enumerate(target_bits(layer)):
        term = ((index >> bits.index(target)) & 1) << j
        code = term if code is None else code + term
    return code


def rest_position(layer, bits):
    targets = target_bits(layer)
    return [i for i, bit in enumerate(bits) if bit not in targets][0]


def holder(z):
    return ((z & 3) << 1) + 1 - (z >> 2)


def picks(layer, bits):
    row = lax.broadcasted_iota(jnp.int32, (256, 128), 0)
    column = lax.broadcasted_iota(jnp.int32, (256, 128), 1)
    code = gate_code(row & 127, layer, bits) + ((row >> 7) << 6)
    return (code == column).astype(F32).astype(BF16)


def rest_mask(layer, bits):
    i = lax.broadcasted_iota(jnp.int32, (128, 128), 0)
    j = lax.broadcasted_iota(jnp.int32, (128, 128), 1)
    return (((i ^ j) >> rest_position(layer, bits)) & 1) == 0


def spread_gate(u, layer, bits, picked, mask, on_rows):
    row = lax.broadcasted_iota(jnp.int32, (128, 64), 0)
    column = lax.broadcasted_iota(jnp.int32, (128, 64), 1)
    chooser = (gate_code(row, layer, bits) == column).astype(F32).astype(BF16)
    u_parts = halves(u)
    tall = jnp.concatenate([mm(chooser, part, NN).astype(BF16) for part in u_parts], 0)
    out = []
    if on_rows:
        wide = mm(picked, tall, NT)
        for part in range(2):
            columns = slice(128 * part, 128 * part + 128)
            real = jnp.where(mask, wide[:128, columns], 0.0)
            imag = jnp.where(mask, wide[128:, columns], 0.0)
            out.append(jnp.concatenate([jnp.concatenate([real, imag], 1), jnp.concatenate([-imag, real], 1)], 0).astype(BF16))
    else:
        wide = mm(tall, picked, NT)
        for part in range(2):
            rows = slice(128 * part, 128 * part + 128)
            real = jnp.where(mask, wide[rows, :128], 0.0)
            imag = jnp.where(mask, wide[rows, 128:], 0.0)
            out.append(jnp.concatenate([jnp.concatenate([real, -imag], 1), jnp.concatenate([imag, real], 1)], 0).astype(BF16))
    return tuple(out)


def undo_on_rows(gate, x):
    flat = jnp.concatenate([jnp.concatenate([x[0], x[2]], 1), jnp.concatenate([x[1], x[3]], 1)], 0)
    y = mm3(gate, halves(flat), NN)
    return [y[:128, :128], y[128:, :128], y[:128, 128:], y[128:, 128:]]


def undo_on_lanes(gate, x):
    flat = jnp.concatenate([jnp.concatenate([x[0], x[1]], 1), jnp.concatenate([x[2], x[3]], 1)], 0)
    y = mm3(halves(flat), gate, NN)
    return [y[:128, :128], y[:128, 128:], y[128:, :128], y[128:, 128:]]


def outer_on_rows(bra, ket):
    left = jnp.concatenate(bra, 1)
    right = jnp.concatenate([jnp.concatenate([ket[0], ket[1]], 1), jnp.concatenate([ket[1], -ket[0]], 1)], 0)
    return mm3(halves(left), halves(right), NT)


def outer_on_lanes(bra, ket):
    left = jnp.concatenate(bra, 0)
    right = jnp.concatenate([jnp.concatenate([ket[0], ket[1]], 1), jnp.concatenate([ket[1], -ket[0]], 1)], 0)
    return mm3(halves(left), halves(right), TN)


def to_chunks(wide, layer, bits, picked, mask, slot, by_plane):
    kept = jnp.concatenate([jnp.where(mask, wide[:, :128], 0.0), jnp.where(mask, wide[:, 128:], 0.0)], 1)
    both = mm(jnp.concatenate(halves(kept), 0), picked, NN)
    narrow = jnp.concatenate(halves(both[:128] + both[128:]), 0)
    shape = (256 if by_plane else 64, 256)
    row = lax.broadcasted_iota(jnp.int32, shape, 0)
    column = lax.broadcasted_iota(jnp.int32, shape, 1)
    code = gate_code(column & 127, layer, bits)
    if by_plane:
        place = (((code & 8) + holder(code & 7)) << 4) + ((code >> 5) << 3) + (((code >> 4) & 1) << 2) + slot
    else:
        place = (holder(code & 7) << 3) + (code >> 3)
    return mm((row == place).astype(F32).astype(BF16), narrow, NN)


def swap_lane(x, row_bit, lane_bit):
    size, step = 1 << row_bit, 1 << lane_bit
    lane = lax.broadcasted_iota(jnp.int32, (size, 128), 1)
    upper = ((lane >> lane_bit) & 1) == 1
    out = []
    for base in range(0, 128, 2 * size):
        a, b = x[base : base + size], x[base + size : base + 2 * size]
        out.append(jnp.where(upper, pltpu.roll(b, step, 1), a))
        out.append(jnp.where(upper, b, pltpu.roll(a, 128 - step, 1)))
    return jnp.concatenate(out, 0)


def swap_sublane(x, row_bit):
    upper = lax.broadcasted_iota(jnp.int32, (8, 128), 0) >= 4
    tiles = [x[8 * i : 8 * i + 8] for i in range(16)]
    bit = 1 << (row_bit - 3)
    out = [None] * 16
    for i in range(16):
        if not i & bit:
            a, b = tiles[i], tiles[i | bit]
            out[i] = jnp.where(upper, pltpu.roll(b, 4, 0), a)
            out[i | bit] = jnp.where(upper, b, pltpu.roll(a, 4, 0))
    return jnp.concatenate(out, 0)


def hops(k):
    in_y = 1 if k & 1 else (2 if k & 16 else 0)
    in_x = 1 if k & 4 else (2 if k & 8 else 0)
    return 2 * (in_x + in_y) + ((k >> 1) & 1)


IN_PLANE = sorted(range(1, 32), key=hops, reverse=True)
IN_LINE = [k >> 1 for k in IN_PLANE if k < 16 and not k & 1]


def kernel(
    scale, ket_ref, bra_ref, gate_hbm, outs,
    states, gates, send_a, recv_a, send_b, recv_b, chunks, partial, packed, column,
    line_out, line_in, rows_out, rows_in, extra, share, final,
    in_sem, a_send, a_recv, b_send, b_recv, c_send, c_recv, z_send, z_recv, l_send, l_recv, q_send, q_recv, f_send, f_recv, line, near, mid, far,
):
    hi, lo = lax.axis_index("hi"), lax.axis_index("lo")
    z, y = lo & 31, lo >> 5
    me = hi * 2 + y
    held = ((hi & 7) >> 1) + ((1 - (hi & 1)) << 2)
    loads = [
        pltpu.make_async_copy(gate_hbm, gates, in_sem.at[2]),
        pltpu.make_async_copy(ket_ref, states.at[0], in_sem.at[0]),
        pltpu.make_async_copy(bra_ref, states.at[1], in_sem.at[1]),
    ]
    for load in loads:
        load.start()

    def ring(step):
        return (hi, (lo & 32) + ((z + step) & 31))

    def in_plane(k):
        return (hi ^ (k >> 1), lo ^ ((k & 1) * 32))

    barrier = pltpu.get_barrier_semaphore()

    def greet(device):
        pl.semaphore_signal(barrier, inc=1, device_id=device, device_id_type=MESH)

    greet((hi ^ 4, lo ^ 2))
    for step in (2, -2, 1, -1):
        greet(ring(step))
    for k in IN_LINE:
        greet((hi ^ k, lo))
    for k in (16, 17, 1):
        greet(in_plane(k))
    extra[...] = jnp.zeros((2, 8, 128), F32)
    loads[0].wait()

    def layer_setup(layer, bits, on_rows):
        picked, mask = picks(layer, bits), rest_mask(layer, bits)
        return picked, mask, spread_gate(gates[layer], layer, bits, picked, mask, on_rows)

    pick4, mask4, gate4 = layer_setup(4, ROWS, True)
    pick3, mask3, gate3 = layer_setup(3, LANES, False)

    loads[1].wait()
    loads[2].wait()
    x5 = [swap_sublane(states[s, pl.ds(c, 128, stride=2), :], 6) for s in range(2) for c in range(2)]
    x4 = undo_on_rows(gate4, x5)
    x3 = undo_on_lanes(gate3, x4)
    mine = ((hi >> 2) & 1) * 2 + ((lo >> 1) & 1)
    for i in range(4):
        ready = swap_lane(x3[i], 5, 3)
        for block in range(4):
            send_a[block, i] = ready[32 * block : 32 * block + 32]

    pl.semaphore_wait(barrier, 15)

    def copy_a(d):
        return pltpu.make_async_remote_copy(
            send_a.at[mine ^ d], recv_a.at[mine], a_send.at[d], a_recv.at[d],
            device_id=(hi ^ (4 if d & 2 else 0), lo ^ (2 if d & 1 else 0)), device_id_type=MESH,
        )

    copy_a(1).start()
    copy_a(3).start()
    copy_a(2).start()
    for k in IN_LINE:
        pl.semaphore_signal(line, inc=1, device_id=(hi ^ k, lo), device_id_type=MESH)
    for step in (2, -2):
        pl.semaphore_signal(near, inc=1, device_id=ring(step), device_id_type=MESH)
    recv_a[mine] = send_a[mine]

    def all_of(ref, sem):
        pltpu.make_async_copy(ref, ref, sem).wait()

    first = to_chunks(outer_on_rows(x5[2:], x4[:2]), 4, ROWS, pick4, mask4, 0, True)
    first += to_chunks(outer_on_lanes(x4[2:], x3[:2]), 3, LANES, pick3, mask3, 3, True)
    chunks[...] = first.reshape(32, 8, 128)
    partial[me] = chunks[me]
    pl.semaphore_wait(line, 7)
    pl.semaphore_wait(near, 2)
    for step in (4, -4):
        pl.semaphore_signal(mid, inc=1, device_id=ring(step), device_id_type=MESH)
    for k in IN_PLANE:
        pltpu.make_async_remote_copy(
            chunks.at[me ^ k], partial.at[me], c_send, c_recv, device_id=in_plane(k), device_id_type=MESH,
        ).start()

    pick2, mask2, gate2 = layer_setup(2, ROWS_MIXED, True)
    pick1, mask1, gate1 = layer_setup(1, LANES, False)
    pick0, mask0, gate0 = layer_setup(0, ROWS, True)
    pl.semaphore_wait(mid, 2)
    for step in (8, -8):
        pl.semaphore_signal(far, inc=1, device_id=ring(step), device_id_type=MESH)

    for d in (1, 2, 3):
        copy_a(d).wait()
    x = [jnp.concatenate([recv_a[block, i] for block in range(4)], 0) for i in range(4)]
    x = [swap_lane(v, 5, 3) for v in x]
    mixed = [swap_lane(swap_lane(swap_lane(v, 3, 4), 4, 5), 5, 6) for v in x]

    def send_line(layer, value):
        line_out[layer] = value.reshape(8, 8, 128)
        for k in IN_LINE:
            pltpu.make_async_remote_copy(
                line_out.at[layer, (hi & 7) ^ k], line_in.at[layer, hi & 7], l_send.at[layer], l_recv.at[layer],
                device_id=(hi ^ k, lo), device_id_type=MESH,
            ).start()
        line_in[layer, hi & 7] = line_out[layer, hi & 7]

    x2 = undo_on_rows(gate2, mixed)
    turned = [swap_lane(swap_lane(swap_lane(v, 3, 4), 4, 5), 5, 6) for v in x2]
    x1 = undo_on_lanes(gate1, turned)
    send_line(2, to_chunks(outer_on_rows(mixed[2:], x2[:2]), 2, ROWS_MIXED, pick2, mask2, 0, False))
    x0 = undo_on_rows(gate0, x1)
    send_line(1, to_chunks(outer_on_lanes(turned[2:], x1[:2]), 1, LANES, pick1, mask1, 0, False))
    send_line(0, to_chunks(outer_on_rows(x1[2:], x0[:2]), 0, ROWS, pick0, mask0, 0, False))

    own = ((hi >> 1) & 1) * 4 + (lo & 1) * 2 + (hi & 1)
    for i in range(4):
        ready = swap_sublane(swap_lane(swap_lane(x0[i], 5, 6), 4, 0), 3)
        for block in range(8):
            for top in range(2):
                send_b[block, i, top] = ready[64 * top + 8 * block : 64 * top + 8 * block + 8]
    recv_b[own] = send_b[own]
    copies_b = []
    for d in range(1, 8):
        copy = pltpu.make_async_remote_copy(
            send_b.at[own ^ d], recv_b.at[own], b_send.at[d], b_recv.at[d],
            device_id=(hi ^ ((2 if d & 4 else 0) + (d & 1)), lo ^ (1 if d & 2 else 0)), device_id_type=MESH,
        )
        copy.start()
        copies_b.append(copy)

    sub = lax.broadcasted_iota(jnp.int32, (8, 128), 0)
    all_of(partial.at[pl.ds(0, 31)], c_recv)
    sum1 = jnp.sum(partial[...], 0)
    turned1 = pltpu.roll(sum1, 4, 0)
    for q in range(2):
        three, four = (turned1, sum1) if q else (sum1, turned1)
        packed[q] = jnp.where(sub == 3, three, jnp.where(sub == 4, four, 0.0))
    pl.semaphore_wait(far, 2)

    def column_copy(q):
        return pltpu.make_async_remote_copy(
            packed.at[q], column.at[z], z_send.at[q], z_recv,
            device_id=(hi, (lo & 32) + held + (hi & 8) + 16 * q), device_id_type=MESH,
        )

    sums = []
    for layer in (2, 1, 0):
        all_of(line_in.at[layer, pl.ds(0, 7)], l_recv.at[layer])
        sums.insert(0, jnp.sum(line_in[layer], 0))
    for q in range(4):
        value = jnp.zeros((8, 128), F32)
        for layer in range(3):
            shift = (layer - q) % 8
            value = jnp.where(sub & 3 == layer, pltpu.roll(sums[layer], shift, 0) if shift else sums[layer], value)
        rows_out[q] = value

    def row_copy(q):
        return pltpu.make_async_remote_copy(
            rows_out.at[q], rows_in.at[z], q_send.at[q], q_recv,
            device_id=(hi, (lo & 32) + held + 8 * q), device_id_type=MESH,
        )

    for q in range(4):
        @pl.when(z != held + 8 * q)
        def _():
            row_copy(q).start()

        @pl.when(z == held + 8 * q)
        def _():
            rows_in[z] = rows_out[q]

    for q in range(2):
        @pl.when(z != held + (hi & 8) + 16 * q)
        def _():
            column_copy(q).start()

        @pl.when(z == held + (hi & 8) + 16 * q)
        def _():
            column[z] = packed[q]

    for copy in copies_b:
        copy.wait()
    for i in range(4):
        v = jnp.concatenate([recv_b[block, i, top] for top in range(2) for block in range(8)], 0)
        v = swap_lane(swap_lane(swap_sublane(v, 3), 4, 0), 5, 6)
        outs[pl.ds(256 * (i // 2) + i % 2, 128, stride=2), :] = swap_sublane(v, 6)
    all_of(chunks.at[pl.ds(0, 31)], c_send)
    for layer in range(3):
        all_of(line_out.at[layer, pl.ds(0, 7)], l_send.at[layer])
    for q in range(2):
        @pl.when(z != held + (hi & 8) + 16 * q)
        def _():
            column_copy(q).wait_send()

    for q in range(4):
        @pl.when(z != held + 8 * q)
        def _():
            row_copy(q).wait_send()

    sink = (z & 7) == held
    slot = (hi >> 3) * 2 + y

    @pl.when((z & 15) == held + (hi & 8))
    def _():
        all_of(column.at[pl.ds(0, 31)], z_recv)
        extra[y] = jnp.sum(column[...], 0)

    @pl.when(sink)
    def _():
        all_of(rows_in.at[pl.ds(0, 31)], q_recv)
        total = jnp.sum(rows_in[...], 0)
        share[0] = jnp.where(sub < 3, total, 0.0) + extra[0]
        share[1] = jnp.where(sub < 3, pltpu.roll(total, 4, 0), 0.0) + extra[1]
        for k in IN_PLANE:
            pltpu.make_async_remote_copy(
                share.at[y ^ (k & 1)], final.at[slot], f_send, f_recv, device_id=in_plane(k), device_id_type=MESH,
            ).start()
        final[slot] = share[y]
        all_of(final.at[pl.ds(0, 3)], f_recv)

    @pl.when(jnp.logical_not(sink))
    def _():
        all_of(final.at[pl.ds(0, 4)], f_recv)

    outs[512:520, :] = jnp.sum(final[...], 0) * scale
    @pl.when(sink)
    def _():
        all_of(column.at[pl.ds(0, 31)], f_send)


def put_kernel(whole, ket, bra, grad, slim, sem):
    copies = [
        pltpu.make_async_copy(whole.at[pl.ds(0, 256)], ket, sem.at[0]),
        pltpu.make_async_copy(whole.at[pl.ds(256, 256)], bra, sem.at[1]),
        pltpu.make_async_copy(slim, grad, sem.at[2]),
    ]
    for layer in range(5):
        slim[layer] = whole[512 + layer : 513 + layer, :]
    for copy in copies:
        copy.start()
    for copy in copies:
        copy.wait()


def body(ket_state, bra_state, gate_matrices):
    scale = (64 / (16384 * lax.axis_size("hi") * lax.axis_size("lo"))) ** 0.5
    amplitudes = ket_state.shape[1]
    hbm = pl.BlockSpec(memory_space=pltpu.HBM)
    dma = pltpu.SemaphoreType.DMA
    regular = pltpu.SemaphoreType.REGULAR
    whole = pl.pallas_call(
        functools.partial(kernel, scale),
        out_shape=jax.ShapeDtypeStruct((520, 128), F32),
        in_specs=[hbm] * 3,
        out_specs=pl.BlockSpec(memory_space=pltpu.VMEM),
        scratch_shapes=[
            pltpu.VMEM((2, 256, 128), F32),
            pltpu.VMEM((5, 64, 128), F32),
            pltpu.VMEM((4, 4, 32, 128), F32),
            pltpu.VMEM((4, 4, 32, 128), F32),
            pltpu.VMEM((8, 4, 2, 8, 128), F32),
            pltpu.VMEM((8, 4, 2, 8, 128), F32),
            pltpu.VMEM((32, 8, 128), F32),
            pltpu.VMEM((32, 8, 128), F32),
            pltpu.VMEM((2, 8, 128), F32),
            pltpu.VMEM((32, 8, 128), F32),
            pltpu.VMEM((3, 8, 8, 128), F32),
            pltpu.VMEM((3, 8, 8, 128), F32),
            pltpu.VMEM((4, 8, 128), F32),
            pltpu.VMEM((32, 8, 128), F32),
            pltpu.VMEM((2, 8, 128), F32),
            pltpu.VMEM((2, 8, 128), F32),
            pltpu.VMEM((4, 8, 128), F32),
            dma((3,)), dma((4,)), dma((4,)), dma((8,)), dma((8,)),
            dma, dma, dma((2,)), dma, dma((3,)), dma((3,)), dma((4,)), dma, dma, dma,
            regular, regular, regular, regular,
        ],
        compiler_params=pltpu.CompilerParams(collective_id=0, has_side_effects=True, vmem_limit_bytes=40 * 2**20),
        name="window",
    )(
        *(
            pltpu.with_memory_space_constraint(v, pltpu.HBM)
            for v in (
                ket_state.reshape(2, 128, 128).transpose(1, 0, 2).reshape(256, 128),
                bra_state.reshape(2, 128, 128).transpose(1, 0, 2).reshape(256, 128),
                gate_matrices,
            )
        ),
    )
    state = jax.ShapeDtypeStruct((256, 128), F32)
    slim = jax.ShapeDtypeStruct((5, 1, 128), F32)
    ket, bra, grad = pl.pallas_call(
        put_kernel,
        out_shape=(state, state, slim),
        in_specs=[pl.BlockSpec(memory_space=pltpu.VMEM)],
        out_specs=(hbm,) * 3,
        scratch_shapes=[pltpu.VMEM((5, 1, 128), F32), dma((3,))],
        name="put",
    )(pltpu.with_memory_space_constraint(whole, pltpu.VMEM))
    ket, bra = (v.reshape(128, 2, 128).transpose(1, 0, 2).reshape(2, amplitudes) for v in (ket, bra))
    return ket, bra, grad


def solution(mesh):
    placed = (P(None, ("hi", "lo")), P(None, ("hi", "lo")), P())
    return jax.shard_map(
        body,
        mesh=mesh,
        in_specs=placed,
        out_specs=(P(None, ("hi", "lo")), P(None, ("hi", "lo")), P(None, "lo", None)),
        check_vma=False,
    )
```
